128 devices in a mesh: dp: 8 (over z, x_hi), seq: 16 (over y, x_lo, core).
Axes of the slice: x: 4 (x_hi: 2, x_lo: 2; x = x_hi * 2 + x_lo), y: 4, z: 4, core: 2. Of those that a mesh axis runs over, the one named last changes fastest.
Arguments:
- layer_input: bfloat16 [8, 64, 256, 1152], P('dp', 'seq'), may hold values from -8 to 8
- queries: bfloat16 [8, 64, 256, 1152], P('dp', 'seq'), may hold values from -5 to 5
- keys: bfloat16 [8, 64, 256, 1152], P('dp', 'seq'), may hold values from -5 to 5
- values: bfloat16 [8, 64, 256, 1152], P('dp', 'seq'), may hold values from -6 to 6
- d_attn: bfloat16 [8, 64, 256, 1152], P('dp', 'seq'), may hold values from -6 to 6
- w_qkv: bfloat16 [1152, 3456], replicated, may hold values from -0.1875 to 0.1875
Outputs:
- d_input: bfloat16 [8, 64, 256, 1152], P('dp', 'seq')
- d_weight: float32 [1152, 3456], P('seq')
The draws below stay inside these ranges and needn't reach their ends.
All inputs are finite; a program needn't handle non-finite values.
Results may differ from the reference program's by a relative error of at most 0.0068.
Values may be sent and summed in bfloat16 or wider, within the bound.
No kernel may reach another device: no remote copies, remote signals or barrier semaphores. Data moves between devices by JAX's collectives and lax.ppermute only.
A program may use at most 192 MiB of HBM per device.

```python
import jax
import jax.numpy as jnp
from jax import lax

HEADS = 16
HEAD_DIM = 72
D = 1152
FRAMES = 64
SPATIAL = 256
CLIPS = 8


def base_field(key):
    return jnp.clip(jax.random.normal(key, (CLIPS, FRAMES, SPATIAL, D), jnp.float32), -4.5, 4.5)


def draw_queries(key, part):
    key = jax.random.fold_in(key, 1)
    field = base_field(key)
    return field.astype(jnp.bfloat16)


def draw_keys(key, part):
    key = jax.random.fold_in(key, 2)
    field = base_field(key)
    return field.astype(jnp.bfloat16)


def spiked(values, own_key, source, target, parts, factor):
    def block_of(position):
        return (jnp.arange(values.shape[position]) // (values.shape[position] // parts)).reshape((-1,) + (1,) * (values.ndim - 1 - position))

    near = jax.random.permutation(own_key, parts)[block_of(target)]
    far = (block_of(target) + parts // 2) % parts
    return jnp.where((block_of(source) == near) | (block_of(source) == far), factor * values, values)


def levels(stream_key, shape, split, low, top_value):
    gain = 1.0
    for axis_at, blocks in split:
        steps = jax.random.uniform(jax.random.fold_in(jax.random.fold_in(stream_key, 6), axis_at), (blocks,), jnp.float32, low / len(split), top_value / len(split))
        gain = gain * jnp.repeat(jnp.exp(steps), shape[axis_at] // blocks).reshape((-1,) + (1,) * (len(shape) - 1 - axis_at))
    return gain


def normal_values(key, shape, width, reach, cuts=(), kind=jnp.bfloat16):
    factor_of = levels(key, shape, cuts, -0.22, 0.18) if cuts else 1.0
    entries = jax.random.normal(key, shape, jnp.float32) * width * factor_of
    return jnp.minimum(jnp.maximum(entries, -reach), reach).astype(kind)


def gaussian_with(key, dims, width, reach, split, heavy, dtype=jnp.bfloat16):
    values = width * jax.random.normal(key, dims, jnp.float32)
    if split:
        values = values * levels(key, dims, split, -0.22, 0.18)
    return jnp.clip(spiked(values, jax.random.fold_in(key, 3), *heavy), -reach, reach).astype(dtype)


def setup_inputs(seed: int = 0) -> dict:
    seeds = jax.random.split(jax.random.key(seed), 7)
    layer_input = gaussian_with(seeds[0], (CLIPS, FRAMES, SPATIAL, D), 1.0, 8.0, ((0, 8), (1, 16)), (1, 3, 16, 2.0))
    queries = draw_queries(jax.random.fold_in(seeds[6], 71), 0)
    keys = draw_keys(jax.random.fold_in(seeds[6], 71), 0)
    values = normal_values(seeds[3], (CLIPS, FRAMES, SPATIAL, D), 1.0, 6.0, ((0, 8), (1, 16)))
    d_attn = normal_values(seeds[4], (CLIPS, FRAMES, SPATIAL, D), 1.0, 6.0, ((0, 8), (1, 16)))
    w_qkv = normal_values(seeds[5], (D, 3 * D), D ** -0.5, 0.1875)
    return dict(layer_input=layer_input, queries=queries, keys=keys, values=values, d_attn=d_attn, w_qkv=w_qkv)


def clip_step(carry, blocks):
    input_clip, q_clip, k_clip, v_clip, d_clip, w_qkv = blocks
    factor = HEAD_DIM ** (-0.5)
    shape4 = (FRAMES, SPATIAL, HEADS, HEAD_DIM)
    q_f = q_clip.reshape(shape4).astype(jnp.float32)
    k_f = k_clip.reshape(shape4).astype(jnp.float32)
    v_f = v_clip.reshape(shape4).astype(jnp.float32)
    d_f = d_clip.reshape(shape4).astype(jnp.float32)
    scores = jnp.einsum('fshd,gshd->fgsh', q_f, k_f) * factor
    maxima = lax.optimization_barrier(jnp.max(scores, axis=1, keepdims=True))
    exp_term = jnp.exp(scores - maxima)
    probability = exp_term / lax.optimization_barrier(jnp.sum(exp_term, axis=1, keepdims=True))
    prob_low = probability.astype(jnp.bfloat16).astype(jnp.float32)
    output = jnp.einsum('fgsh,gshd->fshd', prob_low, v_f)
    delta_row = lax.optimization_barrier(jnp.sum(d_f * output, axis=-1))
    grad_v = jnp.einsum('fgsh,fshd->gshd', prob_low, d_f).astype(jnp.bfloat16)
    grad_p = jnp.einsum('fshd,gshd->fgsh', d_f, v_f)
    grad_s = (probability * (grad_p - delta_row[:, None])).astype(jnp.bfloat16).astype(jnp.float32)
    grad_q = (jnp.einsum('fgsh,gshd->fshd', grad_s, k_f) * factor).astype(jnp.bfloat16)
    grad_k = (jnp.einsum('fgsh,fshd->gshd', grad_s, q_f) * factor).astype(jnp.bfloat16)
    tokens_all = FRAMES * SPATIAL
    grad_all = jnp.concatenate([grad_q.reshape(tokens_all, D), grad_k.reshape(tokens_all, D), grad_v.reshape(tokens_all, D)], axis=1)
    d_clip_in = jnp.dot(grad_all, w_qkv.T, preferred_element_type=jnp.float32).astype(jnp.bfloat16)
    flat_input = input_clip.reshape(tokens_all, D)
    term = jnp.dot(flat_input.T, grad_all, preferred_element_type=jnp.float32)
    return (carry + term, d_clip_in.reshape(FRAMES, SPATIAL, D))

def reference(layer_input, queries, keys, values, d_attn, w_qkv):

    def stepper(carry, blocks):
        return clip_step(carry, blocks + (w_qkv,))
    start = jnp.zeros((D, 3 * D), jnp.float32)
    total, d_input = lax.scan(stepper, start, (layer_input, queries, keys, values, d_attn))
    d_weight = total / jnp.sqrt(jnp.float32(CLIPS * FRAMES * SPATIAL))
    return (d_input, d_weight)
```

```python
import functools
import math

import jax
import jax.numpy as jnp
from jax import lax
from jax.experimental import pallas as pl
from jax.experimental.pallas import tpu as pltpu
from jax.sharding import Mesh
from jax.sharding import PartitionSpec as P

HEADS = 16
HEAD_DIM = 72
FRAMES = 64
SPATIAL = 256
WIDTH = HEADS * HEAD_DIM
LANES = 128
TILES = WIDTH // LANES
FACTOR = HEAD_DIM ** (-0.5)
SEQ = ("y", "xl", "core")
PIECES = ((0, 512), (2048, 384))
MIB = 1024 * 1024


def pack_kernel(*refs):
    out_ref = refs[-1]
    for n, ref in enumerate(refs[:-1]):
        out_ref[0, n] = ref[0]


def pack(arrays, devices):
    frames, cells = arrays[0].shape[1], arrays[0].shape[2] // devices
    block = pl.BlockSpec((1, frames, cells, WIDTH), lambda j: (0, 0, j, 0))
    count = len(arrays)
    return pl.pallas_call(
        pack_kernel,
        grid=(devices,),
        in_specs=[block] * count,
        out_specs=pl.BlockSpec((1, count, frames, cells, WIDTH), lambda j: (j, 0, 0, 0, 0)),
        out_shape=jax.ShapeDtypeStruct((devices, count, frames, cells, WIDTH), jnp.bfloat16),
        compiler_params=pltpu.CompilerParams(vmem_limit_bytes=32 * MIB),
        cost_estimate=pl.CostEstimate(
            flops=0, bytes_accessed=2 * count * arrays[0].size * 2, transcendentals=0
        ),
    )(*arrays)


def unpack_kernel(in_ref, out_ref):
    out_ref[0] = in_ref[0]


def unpack(blocks):
    devices, frames, cells, width = blocks.shape
    return pl.pallas_call(
        unpack_kernel,
        grid=(devices,),
        in_specs=[pl.BlockSpec((1, frames, cells, width), lambda j: (j, 0, 0, 0))],
        out_specs=pl.BlockSpec((1, frames, cells, width), lambda j: (0, 0, j, 0)),
        out_shape=jax.ShapeDtypeStruct((1, frames, cells * devices, width), jnp.bfloat16),
        compiler_params=pltpu.CompilerParams(vmem_limit_bytes=32 * MIB),
        cost_estimate=pl.CostEstimate(flops=0, bytes_accessed=4 * blocks.size, transcendentals=0),
    )(blocks)


def dot_nt(a, b):
    return lax.dot_general(a, b, (((1,), (1,)), ((), ())), preferred_element_type=jnp.float32)


def dot_tn(a, b):
    return lax.dot_general(a, b, (((0,), (0,)), ((), ())), preferred_element_type=jnp.float32)


def dot_nn(a, b):
    return jnp.dot(a, b, preferred_element_type=jnp.float32)


def attend_kernel(cells, r_ref, g_ref, q_scr, k_scr, v_scr, d_scr):
    rows = FRAMES * cells
    scratches = (q_scr, k_scr, v_scr, d_scr)
    for n, scr in enumerate(scratches):
        for t in range(TILES):
            tile = r_ref[:, n, :, :, t * LANES : (t + 1) * LANES]
            scr[t] = tile.reshape(rows, LANES).astype(jnp.float32)

    pair_rows = 2 * FRAMES
    same = (lax.broadcasted_iota(jnp.int32, (pair_rows, pair_rows), 0) < FRAMES) == (
        lax.broadcasted_iota(jnp.int32, (pair_rows, pair_rows), 1) < FRAMES
    )

    def pair_step(i, carry):
        p = 2 * i

        def load(scr, t):
            first = scr[t, pl.ds(p, FRAMES, stride=cells), :]
            second = scr[t, pl.ds(p + 1, FRAMES, stride=cells), :]
            return jnp.concatenate([first, second], axis=0).astype(jnp.bfloat16)

        q_t, k_t, v_t, d_t = ([load(scr, t) for t in range(TILES)] for scr in scratches)
        acc = [dict(), dict(), dict()]

        def put(n, t, value):
            acc[n][t] = acc[n][t] + value if t in acc[n] else value

        for h in range(HEADS):
            start = h * HEAD_DIM
            first = start // LANES
            last = (start + HEAD_DIM - 1) // LANES
            tiles = range(first, last + 1)
            low = start - first * LANES
            lane = lax.broadcasted_iota(jnp.int32, (1, LANES * len(tiles)), 1)
            mask = ((lane >= low) & (lane < low + HEAD_DIM)).astype(jnp.bfloat16)

            def window(parts):
                return jnp.concatenate([parts[t] for t in tiles], axis=1)

            q_h = window(q_t) * mask
            k_h = window(k_t) * mask
            d_h = window(d_t) * mask
            v_h = window(v_t)
            scores = jnp.where(same, dot_nt(q_h, k_h) * FACTOR, -1e30)
            top = jnp.max(scores, axis=1, keepdims=True)
            exp_term = jnp.exp(scores - top)
            prob = exp_term / jnp.sum(exp_term, axis=1, keepdims=True)
            prob_low = prob.astype(jnp.bfloat16)
            grad_p = dot_nt(d_h, v_h)
            delta = jnp.sum(prob_low.astype(jnp.float32) * grad_p, axis=1, keepdims=True)
            grad_s = (prob * (grad_p - delta)).astype(jnp.bfloat16)
            results = (
                dot_nn(grad_s, k_h) * FACTOR,
                dot_tn(grad_s, q_h) * FACTOR,
                dot_tn(prob_low, d_h),
            )
            for n, result in enumerate(results):
                for at, t in enumerate(tiles):
                    put(n, t, result[:, at * LANES : (at + 1) * LANES])
            done = TILES if h == HEADS - 1 else (start + HEAD_DIM) // LANES
            for t in range(first, done):
                for n, scr in enumerate((q_scr, k_scr, v_scr)):
                    value = acc[n].pop(t)
                    scr[t, pl.ds(p, FRAMES, stride=cells), :] = value[:FRAMES]
                    scr[t, pl.ds(p + 1, FRAMES, stride=cells), :] = value[FRAMES:]
        return carry

    lax.fori_loop(0, cells // 2, pair_step, 0)
    for n, scr in enumerate((q_scr, k_scr, v_scr)):
        for t in range(TILES):
            lo = n * WIDTH + t * LANES
            g_ref[:, lo : lo + LANES] = scr[t].astype(jnp.bfloat16)


def attend(received):
    devices, _, frames, cells, _ = received.shape
    rows = devices * frames * cells
    scratch = pltpu.VMEM((TILES, rows, LANES), jnp.float32)
    return pl.pallas_call(
        functools.partial(attend_kernel, cells),
        in_specs=[pl.BlockSpec(memory_space=pltpu.VMEM)],
        out_specs=pl.BlockSpec(memory_space=pltpu.VMEM),
        out_shape=jax.ShapeDtypeStruct((rows, 3 * WIDTH), jnp.bfloat16),
        scratch_shapes=[scratch] * 4,
        compiler_params=pltpu.CompilerParams(vmem_limit_bytes=56 * MIB),
        cost_estimate=pl.CostEstimate(
            flops=20_000_000_000, bytes_accessed=14 * rows * WIDTH, transcendentals=4_000_000
        ),
    )(received)


def input_grad_kernel(g_ref, w_ref, out_ref):
    out_ref[...] = dot_nt(g_ref[...], w_ref[...]).astype(jnp.bfloat16)


def input_grad(grads, weight):
    rows, depth = grads.shape
    step = 384
    return pl.pallas_call(
        input_grad_kernel,
        grid=(WIDTH // step,),
        in_specs=[
            pl.BlockSpec((rows, depth), lambda j: (0, 0)),
            pl.BlockSpec((step, depth), lambda j: (j, 0)),
        ],
        out_specs=pl.BlockSpec((rows, step), lambda j: (0, j)),
        out_shape=jax.ShapeDtypeStruct((rows, WIDTH), jnp.bfloat16),
        compiler_params=pltpu.CompilerParams(vmem_limit_bytes=56 * MIB),
        cost_estimate=pl.CostEstimate(
            flops=2 * rows * depth * WIDTH, bytes_accessed=2 * depth * (rows + WIDTH), transcendentals=0
        ),
    )(grads, weight)


def weight_grad_kernel(first, step, owners, core_ref, x_ref, g_ref, out_ref, xt_scr):
    @pl.when(pl.program_id(0) == 0)
    def _():
        xt_scr[...] = x_ref[...].T

    share = WIDTH // (2 * owners)
    part = dot_nn(xt_scr[...], g_ref[...])
    for block in range(owners):
        for c in range(2):
            lo = (2 * block + c) * share
            out_ref[c ^ core_ref[0], 0, block] = part[lo : lo + share].astype(jnp.bfloat16)


def weight_grad(core, tokens, grads, first, step, parts, owners):
    rows = tokens.shape[0]
    share = WIDTH // (2 * owners)
    return pl.pallas_call(
        functools.partial(weight_grad_kernel, first, step, owners),
        grid_spec=pltpu.PrefetchScalarGridSpec(
            num_scalar_prefetch=1,
            grid=(parts,),
            in_specs=[
                pl.BlockSpec((rows, WIDTH), lambda j, c: (0, 0)),
                pl.BlockSpec((rows, step), lambda j, c: (0, j)),
            ],
            out_specs=pl.BlockSpec((2, 1, owners, share, step), lambda j, c: (0, j, 0, 0, 0)),
            scratch_shapes=[pltpu.VMEM((WIDTH, rows), jnp.bfloat16)],
        ),
        out_shape=jax.ShapeDtypeStruct((2, parts, owners, share, step), jnp.bfloat16),
        compiler_params=pltpu.CompilerParams(vmem_limit_bytes=56 * MIB),
        cost_estimate=pl.CostEstimate(
            flops=2 * rows * WIDTH * step * parts,
            bytes_accessed=2 * rows * (WIDTH + step * parts) + 2 * WIDTH * step * parts,
            transcendentals=0,
        ),
    )(core, tokens, grads)


def swap(value, axis):
    return lax.ppermute(value, axis, [(0, 1), (1, 0)])


def reduce_piece(part):
    kept = part[0].astype(jnp.float32) + swap(part[1], "core").astype(jnp.float32)
    over_z = lax.psum_scatter(
        kept.astype(jnp.bfloat16), "z", scatter_dimension=0, tiled=True
    )[0]
    blocks = lax.all_to_all(over_z, ("y", "xl"), 0, 0, tiled=True)
    total = jnp.sum(blocks.astype(jnp.float32), axis=0).astype(jnp.bfloat16)
    total = (total.astype(jnp.float32) + swap(total, "xh").astype(jnp.float32)).astype(jnp.bfloat16)
    return lax.all_gather(total, "z", axis=0)


def per_device(layer_input, queries, keys, values, d_attn, w_qkv):
    devices = lax.axis_size(SEQ)
    parts = lax.axis_size("z")
    owners = devices // lax.axis_size("core")
    clips = parts * lax.axis_size("xh")
    frames, spatial = layer_input.shape[1], layer_input.shape[2]
    cells = spatial // devices
    rows = devices * frames * cells
    norm_scale = 1.0 / math.sqrt(clips * FRAMES * SPATIAL)
    core = lax.axis_index("core").reshape(1).astype(jnp.int32)

    sent = pack([queries, keys, values, d_attn], devices)
    received = lax.all_to_all(sent, SEQ, 0, 0, tiled=True)
    sent_x = pack([layer_input], devices)
    tokens = lax.all_to_all(sent_x, SEQ, 0, 0, tiled=True).reshape(rows, WIDTH)

    grads = attend(received)
    d_local = input_grad(grads, w_qkv).reshape(devices, frames, cells, WIDTH)
    d_input = unpack(lax.all_to_all(d_local, SEQ, 0, 0, tiled=True))

    columns = []
    for first, step in PIECES:
        piece = lax.slice_in_dim(grads, first, min(first + parts * step, 3 * WIDTH), axis=1)
        part = weight_grad(core, tokens, piece, first, step, parts, owners)
        gathered = reduce_piece(part)
        for z in range(parts):
            lo = first + z * step
            keep = min(step, 3 * WIDTH - lo)
            columns.append(gathered[z, :, :keep])
    d_weight = jnp.concatenate(columns, axis=1).astype(jnp.float32) * norm_scale
    return (d_input, d_weight)


def solution(mesh):
    sizes = (4, 2, 4, 2, 2)
    fine = Mesh(mesh.devices.reshape(sizes), ("z", "xh", "y", "xl", "core"))
    dp = ("z", "xh")
    block = P(dp, SEQ, None, None)
    return jax.shard_map(
        per_device,
        mesh=fine,
        in_specs=(block,) * 5 + (P(),),
        out_specs=(block, P(SEQ, None)),
        check_vma=False,
    )
```

```python
import functools
import math

import jax
import jax.numpy as jnp
from jax import lax
from jax.experimental import pallas as pl
from jax.experimental.pallas import tpu as pltpu
from jax.sharding import Mesh
from jax.sharding import PartitionSpec as P

HEADS = 16
HEAD_DIM = 72
FRAMES = 64
SPATIAL = 256
WIDTH = HEADS * HEAD_DIM
LANES = 128
TILES = WIDTH // LANES
FACTOR = HEAD_DIM ** (-0.5)
SEQ = ("y", "xl", "core")
MIB = 1024 * 1024


def pack_kernel(cells, group, *refs):
    out_ref = refs[-1]
    for n, ref in enumerate(refs[:-1]):
        for i in range(group):
            out_ref[i, n] = ref[0, :, i * cells : (i + 1) * cells, :]


def pack(arrays, devices):
    frames, cells = arrays[0].shape[1], arrays[0].shape[2] // devices
    group = 4
    block = pl.BlockSpec((1, frames, group * cells, WIDTH), lambda j: (0, 0, j, 0))
    count = len(arrays)
    return pl.pallas_call(
        functools.partial(pack_kernel, cells, group),
        grid=(devices // group,),
        in_specs=[block] * count,
        out_specs=pl.BlockSpec((group, count, frames, cells, WIDTH), lambda j: (j, 0, 0, 0, 0)),
        out_shape=jax.ShapeDtypeStruct((devices, count, frames, cells, WIDTH), jnp.bfloat16),
        compiler_params=pltpu.CompilerParams(vmem_limit_bytes=60 * MIB),
        cost_estimate=pl.CostEstimate(
            flops=0, bytes_accessed=2 * count * arrays[0].size * 2, transcendentals=0
        ),
    )(*arrays)


def unpack_kernel(cells, group, in_ref, out_ref):
    for i in range(group):
        out_ref[0, :, i * cells : (i + 1) * cells, :] = in_ref[i]


def unpack(blocks):
    devices, frames, cells, width = blocks.shape
    group = 4
    return pl.pallas_call(
        functools.partial(unpack_kernel, cells, group),
        grid=(devices // group,),
        in_specs=[pl.BlockSpec((group, frames, cells, width), lambda j: (j, 0, 0, 0))],
        out_specs=pl.BlockSpec((1, frames, group * cells, width), lambda j: (0, 0, j, 0)),
        out_shape=jax.ShapeDtypeStruct((1, frames, cells * devices, width), jnp.bfloat16),
        compiler_params=pltpu.CompilerParams(vmem_limit_bytes=60 * MIB),
        cost_estimate=pl.CostEstimate(flops=0, bytes_accessed=4 * blocks.size, transcendentals=0),
    )(blocks)


def dot_nt(a, b):
    return lax.dot_general(a, b, (((1,), (1,)), ((), ())), preferred_element_type=jnp.float32)


def dot_tn(a, b):
    return lax.dot_general(a, b, (((0,), (0,)), ((), ())), preferred_element_type=jnp.float32)


def dot_nn(a, b):
    return jnp.dot(a, b, preferred_element_type=jnp.float32)


def attend_kernel(cells, r_ref, g_ref, q_scr, k_scr, v_scr, d_scr):
    rows = FRAMES * cells
    scratches = (q_scr, k_scr, v_scr, d_scr)
    for n, scr in enumerate(scratches):
        for t in range(TILES):
            tile = r_ref[:, n, :, :, t * LANES : (t + 1) * LANES]
            scr[t] = tile.reshape(rows, LANES).astype(jnp.float32)

    pair_rows = 2 * FRAMES
    lane = lax.broadcasted_iota(jnp.int32, (FRAMES, 2 * pair_rows), 1)
    left = lane % pair_rows < FRAMES

    def compact(block):
        return jnp.where(left, block[:FRAMES], block[FRAMES:])

    def spread(block):
        zero = jnp.zeros_like(block)
        upper = jnp.where(left, block, zero)
        lower = jnp.where(left, zero, block)
        return jnp.concatenate([upper, lower], axis=0).astype(jnp.bfloat16)

    def pair_step(i, carry):
        p = 2 * i

        def load(scr, t):
            first = scr[t, pl.ds(p, FRAMES, stride=cells), :]
            second = scr[t, pl.ds(p + 1, FRAMES, stride=cells), :]
            return jnp.concatenate([first, second], axis=0).astype(jnp.bfloat16)

        q_t, k_t, v_t, d_t = ([load(scr, t) for t in range(TILES)] for scr in scratches)
        acc = [dict(), dict(), dict()]

        def put(n, t, value):
            acc[n][t] = acc[n][t] + value if t in acc[n] else value

        def scores(h):
            start = h * HEAD_DIM
            first = start // LANES
            low = start - first * LANES
            window_lane = lax.broadcasted_iota(jnp.int32, (1, 2 * LANES), 1)
            masks = [
                ((window_lane >= lo) & (window_lane < lo + HEAD_DIM)).astype(jnp.bfloat16)
                for lo in (low, low + HEAD_DIM)
            ]

            def window(parts):
                return jnp.concatenate([parts[first], parts[first + 1]], axis=1)

            def both(value):
                return jnp.concatenate([value * mask for mask in masks], axis=0)

            k_w = window(k_t)
            q_h = both(window(q_t))
            d_h = both(window(d_t))
            raw = compact(dot_nt(k_w, q_h))
            grad_p = compact(dot_nt(window(v_t), d_h))
            return k_w, q_h, d_h, raw, grad_p

        def soft(k_w, q_h, d_h, raw, grad_p):
            exp_term = jnp.exp((raw - jnp.max(raw, axis=0, keepdims=True)) * FACTOR)
            prob = exp_term * (1.0 / jnp.sum(exp_term, axis=0, keepdims=True))
            prob_low = prob.astype(jnp.bfloat16).astype(jnp.float32)
            delta = jnp.sum(prob_low * grad_p, axis=0, keepdims=True)
            grad_s = spread(prob * (grad_p - delta))
            return k_w, q_h, d_h, spread(prob), grad_s

        def grads(h, k_w, q_h, d_h, prob_low, grad_s):
            start = h * HEAD_DIM
            first = start // LANES
            low = start - first * LANES
            window_lane = lax.broadcasted_iota(jnp.int32, (1, 2 * LANES), 1)
            own = (window_lane >= low) & (window_lane < low + 2 * HEAD_DIM)
            from_keys = dot_tn(grad_s, k_w)
            halves = jnp.where(
                window_lane < low + HEAD_DIM, from_keys[:pair_rows], from_keys[pair_rows:]
            )
            results = (
                jnp.where(own, halves, 0.0),
                dot_nn(grad_s, q_h),
                dot_nn(prob_low, d_h),
            )
            for n, result in enumerate(results):
                put(n, first, result[:, :LANES])
                put(n, first + 1, result[:, LANES:])
            for t in range(first, (start + 2 * HEAD_DIM) // LANES):
                for n, scr in enumerate((q_scr, k_scr, v_scr)):
                    value = acc[n].pop(t)
                    scr[t, pl.ds(p, FRAMES, stride=cells), :] = value[:FRAMES]
                    scr[t, pl.ds(p + 1, FRAMES, stride=cells), :] = value[FRAMES:]

        steps = HEADS // 2
        scored, softened = {}, {}
        for at in range(steps + 2):
            if at < steps:
                scored[at] = scores(2 * at)
            if at >= 2:
                grads(2 * (at - 2), *softened.pop(at - 2))
            if 1 <= at <= steps:
                softened[at - 1] = soft(*scored.pop(at - 1))
        return carry

    lax.fori_loop(0, cells // 2, pair_step, 0)
    for n, scr in enumerate((q_scr, k_scr, v_scr)):
        for t in range(TILES):
            lo = n * WIDTH + t * LANES
            scale = 1.0 if n == 2 else FACTOR
            g_ref[:, lo : lo + LANES] = (scr[t] * scale).astype(jnp.bfloat16)


def attend(received):
    devices, _, frames, cells, _ = received.shape
    rows = devices * frames * cells
    scratch = pltpu.VMEM((TILES, rows, LANES), jnp.float32)
    vmem = pl.BlockSpec(memory_space=pltpu.VMEM)
    return pl.pallas_call(
        functools.partial(attend_kernel, cells),
        in_specs=[vmem],
        out_specs=vmem,
        out_shape=jax.ShapeDtypeStruct((rows, 3 * WIDTH), jnp.bfloat16),
        scratch_shapes=[scratch] * 4,
        compiler_params=pltpu.CompilerParams(vmem_limit_bytes=60 * MIB),
        cost_estimate=pl.CostEstimate(
            flops=24_000_000_000, bytes_accessed=14 * rows * WIDTH, transcendentals=4_000_000
        ),
    )(received)


def input_grad_kernel(g_ref, w_ref, after_ref, out_ref):
    half = g_ref.shape[0] // 2
    for lo in (0, half):
        part = dot_nt(g_ref[lo : lo + half, :], w_ref[...])
        out_ref[lo : lo + half, :] = part.astype(jnp.bfloat16)


def input_grad(grads, weight, after):
    rows, depth = grads.shape
    step = 384
    return pl.pallas_call(
        input_grad_kernel,
        grid=(WIDTH // step,),
        in_specs=[
            pl.BlockSpec((rows, depth), lambda j: (0, 0)),
            pl.BlockSpec((step, depth), lambda j: (j, 0)),
            pl.BlockSpec(memory_space=pl.ANY),
        ],
        out_specs=pl.BlockSpec((rows, step), lambda j: (0, j)),
        out_shape=jax.ShapeDtypeStruct((rows, WIDTH), jnp.bfloat16),
        compiler_params=pltpu.CompilerParams(vmem_limit_bytes=60 * MIB),
        cost_estimate=pl.CostEstimate(
            flops=2 * rows * depth * WIDTH,
            bytes_accessed=2 * depth * (rows + WIDTH),
            transcendentals=0,
        ),
    )(grads, weight, after)


def weight_grad_kernel(owners, core_ref, x_ref, g_ref, out_ref, wide_scr, xt_scr):
    share = WIDTH // (2 * owners)

    @pl.when(pl.program_id(0) == 0)
    def _():
        flipped = x_ref[...].astype(jnp.float32).T
        for block in range(owners):
            lo = 2 * block * share
            rows = jnp.where(
                core_ref[0] == 0, flipped[lo : lo + share], flipped[lo + share : lo + 2 * share]
            )
            wide_scr[block * share : (block + 1) * share, :] = rows
        xt_scr[...] = wide_scr[...].astype(jnp.bfloat16)

    part = dot_nn(xt_scr[...], g_ref[...])
    for block in range(owners):
        out_ref[0, block] = part[block * share : (block + 1) * share].astype(jnp.bfloat16)


def weight_grad(core, tokens, grads, parts, step, owners):
    rows = tokens.shape[0]
    share = WIDTH // (2 * owners)
    return pl.pallas_call(
        functools.partial(weight_grad_kernel, owners),
        grid_spec=pltpu.PrefetchScalarGridSpec(
            num_scalar_prefetch=1,
            grid=(parts,),
            in_specs=[
                pl.BlockSpec((rows, WIDTH), lambda j, c: (0, 0)),
                pl.BlockSpec((rows, step), lambda j, c: (0, j)),
            ],
            out_specs=pl.BlockSpec((1, owners, share, step), lambda j, c: (j, 0, 0, 0)),
            scratch_shapes=[
                pltpu.VMEM((WIDTH // 2, rows), jnp.float32),
                pltpu.VMEM((WIDTH // 2, rows), jnp.bfloat16),
            ],
        ),
        out_shape=jax.ShapeDtypeStruct((parts, owners, share, step), jnp.bfloat16),
        compiler_params=pltpu.CompilerParams(vmem_limit_bytes=60 * MIB),
        cost_estimate=pl.CostEstimate(
            flops=rows * WIDTH * step * parts,
            bytes_accessed=2 * rows * (WIDTH + step * parts) + WIDTH * step * parts,
            transcendentals=0,
        ),
    )(core, tokens, grads)


def swap(value, axis):
    return lax.ppermute(value, axis, [(0, 1), (1, 0)])


def add(first, second):
    return (first.astype(jnp.float32) + second.astype(jnp.float32)).astype(jnp.bfloat16)


def fold_kernel(blocks_ref, after_ref, out_ref):
    total = blocks_ref[0].astype(jnp.float32)
    for n in range(1, blocks_ref.shape[0]):
        total = total + blocks_ref[n].astype(jnp.float32)
    out_ref[...] = total.astype(jnp.bfloat16)


def fold(blocks, after):
    vmem = pl.BlockSpec(memory_space=pltpu.VMEM)
    return pl.pallas_call(
        fold_kernel,
        in_specs=[vmem, pl.BlockSpec(memory_space=pl.ANY)],
        out_specs=vmem,
        out_shape=jax.ShapeDtypeStruct(blocks.shape[1:], jnp.bfloat16),
        cost_estimate=pl.CostEstimate(
            flops=blocks.size, bytes_accessed=2 * blocks.size, transcendentals=0
        ),
    )(blocks, after)


def join_kernel(scale, z_ref, *refs):
    out_ref = refs[-1]
    parts = len(refs) - 1
    step = refs[0].shape[1]
    whole = out_ref.shape[1] - (parts - 1) * step
    for n, ref in enumerate(refs[:-1]):
        part = z_ref[0] ^ n
        lo = pl.multiple_of(part * step, LANES)
        out_ref[:, pl.ds(lo, whole)] = ref[:, :whole].astype(jnp.float32) * scale

        @pl.when(part < parts - 1)
        def _():
            rest = pl.multiple_of(part * step + whole, LANES)
            out_ref[:, pl.ds(rest, step - whole)] = ref[:, whole:].astype(jnp.float32) * scale


def join(z, blocks, scale):
    vmem = pl.BlockSpec(memory_space=pltpu.VMEM)
    rows = blocks[0].shape[0]
    return pl.pallas_call(
        functools.partial(join_kernel, scale),
        in_specs=[pl.BlockSpec(memory_space=pltpu.SMEM)] + [vmem] * len(blocks),
        out_specs=vmem,
        out_shape=jax.ShapeDtypeStruct((rows, 3 * WIDTH), jnp.float32),
        cost_estimate=pl.CostEstimate(
            flops=rows * 3 * WIDTH, bytes_accessed=6 * rows * 3 * WIDTH, transcendentals=0
        ),
    )(z, *blocks)


def per_device(layer_input, queries, keys, values, d_attn, w_qkv):
    devices = lax.axis_size(SEQ)
    parts = lax.axis_size("z")
    owners = devices // lax.axis_size("core")
    clips = parts * lax.axis_size("xh")
    frames, spatial = layer_input.shape[1], layer_input.shape[2]
    cells = spatial // devices
    rows = devices * frames * cells
    norm_scale = 1.0 / math.sqrt(clips * FRAMES * SPATIAL)
    core = lax.axis_index("core").reshape(1).astype(jnp.int32)

    sent = pack([queries, keys, values, d_attn], devices)
    received = lax.all_to_all(sent, SEQ, 0, 0, tiled=True)
    sent_x = pack([layer_input], devices)
    tokens = lax.all_to_all(sent_x, SEQ, 0, 0, tiled=True).reshape(rows, WIDTH)

    grads = attend(received)
    step = -(-3 * WIDTH // (parts * LANES)) * LANES
    sent_part = weight_grad(1 - core, tokens, grads, parts, step, owners)
    own_part = weight_grad(core, tokens, grads, parts, step, owners)
    kept = add(own_part, swap(sent_part, "core"))
    over_z = lax.psum_scatter(kept, "z", scatter_dimension=0, tiled=True)[0]

    d_local = input_grad(grads, w_qkv, kept).reshape(devices, frames, cells, WIDTH)
    d_input = unpack(lax.all_to_all(d_local, SEQ, 0, 0, tiled=True))

    share = fold(lax.all_to_all(over_z, ("y", "xl"), 0, 0, tiled=True), d_input)
    share = add(share, swap(share, "xh"))
    blocks = [share] + [
        lax.ppermute(share, "z", [(i, i ^ n) for i in range(parts)]) for n in range(1, parts)
    ]
    d_weight = join(lax.axis_index("z").reshape(1).astype(jnp.int32), blocks, norm_scale)
    return (d_input, d_weight)


def solution(mesh):
    sizes = (4, 2, 4, 2, 2)
    fine = Mesh(mesh.devices.reshape(sizes), ("z", "xh", "y", "xl", "core"))
    dp = ("z", "xh")
    block = P(dp, SEQ, None, None)
    return jax.shard_map(
        per_device,
        mesh=fine,
        in_specs=(block,) * 5 + (P(),),
        out_specs=(block, P(SEQ, None)),
        check_vma=False,
    )
```

```python
import functools
import math

import jax
import jax.numpy as jnp
from jax import lax
from jax.experimental import pallas as pl
from jax.experimental.pallas import tpu as pltpu
from jax.sharding import Mesh
from jax.sharding import PartitionSpec as P

HEADS = 16
HEAD_DIM = 72
FRAMES = 64
SPATIAL = 256
WIDTH = HEADS * HEAD_DIM
LANES = 128
TILES = WIDTH // LANES
FACTOR = HEAD_DIM ** (-0.5)
SEQ = ("y", "xl", "core")
RANGES = ((0, 1792), (1792, 3456))
MIB = 1024 * 1024


def pack_kernel(cells, group, *refs):
    out_ref = refs[-1]
    for n, ref in enumerate(refs[:-1]):
        for i in range(group):
            out_ref[i, n] = ref[0, :, i * cells : (i + 1) * cells, :]


def pack(arrays, devices):
    frames, cells = arrays[0].shape[1], arrays[0].shape[2] // devices
    group = 4
    block = pl.BlockSpec((1, frames, group * cells, WIDTH), lambda j: (0, 0, j, 0))
    count = len(arrays)
    return pl.pallas_call(
        functools.partial(pack_kernel, cells, group),
        grid=(devices // group,),
        in_specs=[block] * count,
        out_specs=pl.BlockSpec((group, count, frames, cells, WIDTH), lambda j: (j, 0, 0, 0, 0)),
        out_shape=jax.ShapeDtypeStruct((devices, count, frames, cells, WIDTH), jnp.bfloat16),
        compiler_params=pltpu.CompilerParams(vmem_limit_bytes=60 * MIB),
        cost_estimate=pl.CostEstimate(
            flops=0, bytes_accessed=2 * count * arrays[0].size * 2, transcendentals=0
        ),
    )(*arrays)


def unpack_kernel(cells, group, in_ref, out_ref):
    for i in range(group):
        out_ref[0, :, i * cells : (i + 1) * cells, :] = in_ref[i]


def unpack(blocks):
    devices, frames, cells, width = blocks.shape
    group = 4
    return pl.pallas_call(
        functools.partial(unpack_kernel, cells, group),
        grid=(devices // group,),
        in_specs=[pl.BlockSpec((group, frames, cells, width), lambda j: (j, 0, 0, 0))],
        out_specs=pl.BlockSpec((1, frames, group * cells, width), lambda j: (0, 0, j, 0)),
        out_shape=jax.ShapeDtypeStruct((1, frames, cells * devices, width), jnp.bfloat16),
        compiler_params=pltpu.CompilerParams(vmem_limit_bytes=60 * MIB),
        cost_estimate=pl.CostEstimate(flops=0, bytes_accessed=4 * blocks.size, transcendentals=0),
    )(blocks)


def dot_nt(a, b):
    return lax.dot_general(a, b, (((1,), (1,)), ((), ())), preferred_element_type=jnp.float32)


def dot_tn(a, b):
    return lax.dot_general(a, b, (((0,), (0,)), ((), ())), preferred_element_type=jnp.float32)


def dot_nn(a, b):
    return jnp.dot(a, b, preferred_element_type=jnp.float32)


def attend_kernel(cells, r_ref, g_ref, q_scr, k_scr, v_scr, d_scr):
    rows = FRAMES * cells
    scratches = (q_scr, k_scr, v_scr, d_scr)
    for n, scr in enumerate(scratches):
        for t in range(TILES):
            tile = r_ref[:, n, :, :, t * LANES : (t + 1) * LANES]
            scr[t] = tile.reshape(rows, LANES).astype(jnp.float32)

    pair_rows = 2 * FRAMES
    lane = lax.broadcasted_iota(jnp.int32, (FRAMES, 2 * pair_rows), 1)
    left = lane % pair_rows < FRAMES

    def compact(block):
        return jnp.where(left, block[:FRAMES], block[FRAMES:])

    def spread(block):
        zero = jnp.zeros_like(block)
        upper = jnp.where(left, block, zero)
        lower = jnp.where(left, zero, block)
        return jnp.concatenate([upper, lower], axis=0).astype(jnp.bfloat16)

    def pair_step(i, carry):
        p = 2 * i

        def load(scr, t):
            first = scr[t, pl.ds(p, FRAMES, stride=cells), :]
            second = scr[t, pl.ds(p + 1, FRAMES, stride=cells), :]
            return jnp.concatenate([first, second], axis=0).astype(jnp.bfloat16)

        q_t, k_t, v_t, d_t = ([load(scr, t) for t in range(TILES)] for scr in scratches)
        acc = [dict(), dict(), dict()]

        def put(n, t, value):
            acc[n][t] = acc[n][t] + value if t in acc[n] else value

        def scores(h):
            start = h * HEAD_DIM
            first = start // LANES
            low = start - first * LANES
            window_lane = lax.broadcasted_iota(jnp.int32, (1, 2 * LANES), 1)
            masks = [
                ((window_lane >= lo) & (window_lane < lo + HEAD_DIM)).astype(jnp.bfloat16)
                for lo in (low, low + HEAD_DIM)
            ]

            def window(parts):
                return jnp.concatenate([parts[first], parts[first + 1]], axis=1)

            def both(value):
                return jnp.concatenate([value * mask for mask in masks], axis=0)

            k_w = window(k_t)
            q_h = both(window(q_t))
            d_h = both(window(d_t))
            raw = compact(dot_nt(k_w, q_h))
            grad_p = compact(dot_nt(window(v_t), d_h))
            return k_w, q_h, d_h, raw, grad_p

        def soft(k_w, q_h, d_h, raw, grad_p):
            exp_term = jnp.exp((raw - jnp.max(raw, axis=0, keepdims=True)) * FACTOR)
            prob = exp_term * (1.0 / jnp.sum(exp_term, axis=0, keepdims=True))
            prob_low = prob.astype(jnp.bfloat16).astype(jnp.float32)
            delta = jnp.sum(prob_low * grad_p, axis=0, keepdims=True)
            grad_s = spread(prob * (grad_p - delta))
            return k_w, q_h, d_h, spread(prob), grad_s

        def grads(h, k_w, q_h, d_h, prob_low, grad_s):
            start = h * HEAD_DIM
            first = start // LANES
            low = start - first * LANES
            window_lane = lax.broadcasted_iota(jnp.int32, (1, 2 * LANES), 1)
            own = (window_lane >= low) & (window_lane < low + 2 * HEAD_DIM)
            from_keys = dot_tn(grad_s, k_w)
            halves = jnp.where(
                window_lane < low + HEAD_DIM, from_keys[:pair_rows], from_keys[pair_rows:]
            )
            results = (
                jnp.where(own, halves, 0.0),
                dot_nn(grad_s, q_h),
                dot_nn(prob_low, d_h),
            )
            for n, result in enumerate(results):
                put(n, first, result[:, :LANES])
                put(n, first + 1, result[:, LANES:])
            for t in range(first, (start + 2 * HEAD_DIM) // LANES):
                for n, scr in enumerate((q_scr, k_scr, v_scr)):
                    value = acc[n].pop(t)
                    scr[t, pl.ds(p, FRAMES, stride=cells), :] = value[:FRAMES]
                    scr[t, pl.ds(p + 1, FRAMES, stride=cells), :] = value[FRAMES:]

        steps = HEADS // 2
        scored, softened = {}, {}
        for at in range(steps + 2):
            if at < steps:
                scored[at] = scores(2 * at)
            if at >= 2:
                grads(2 * (at - 2), *softened.pop(at - 2))
            if 1 <= at <= steps:
                softened[at - 1] = soft(*scored.pop(at - 1))
        return carry

    lax.fori_loop(0, cells // 2, pair_step, 0)
    for n, scr in enumerate((q_scr, k_scr, v_scr)):
        for t in range(TILES):
            lo = n * WIDTH + t * LANES
            scale = 1.0 if n == 2 else FACTOR
            g_ref[:, lo : lo + LANES] = (scr[t] * scale).astype(jnp.bfloat16)


def attend(received):
    devices, _, frames, cells, _ = received.shape
    rows = devices * frames * cells
    scratch = pltpu.VMEM((TILES, rows, LANES), jnp.float32)
    vmem = pl.BlockSpec(memory_space=pltpu.VMEM)
    return pl.pallas_call(
        functools.partial(attend_kernel, cells),
        in_specs=[vmem],
        out_specs=vmem,
        out_shape=jax.ShapeDtypeStruct((rows, 3 * WIDTH), jnp.bfloat16),
        scratch_shapes=[scratch] * 4,
        compiler_params=pltpu.CompilerParams(vmem_limit_bytes=60 * MIB),
        cost_estimate=pl.CostEstimate(
            flops=24_000_000_000, bytes_accessed=14 * rows * WIDTH, transcendentals=4_000_000
        ),
    )(received)


def input_grad_kernel(g_ref, w_ref, after_ref, out_ref):
    out_ref[...] = dot_nt(g_ref[...], w_ref[...]).astype(jnp.bfloat16)


def input_grad(grads, weight, after):
    rows, depth = grads.shape
    step = 256
    return pl.pallas_call(
        input_grad_kernel,
        grid=(rows // step,),
        in_specs=[
            pl.BlockSpec((step, depth), lambda j: (j, 0)),
            pl.BlockSpec((WIDTH, depth), lambda j: (0, 0)),
            pl.BlockSpec(memory_space=pl.ANY),
        ],
        out_specs=pl.BlockSpec((step, WIDTH), lambda j: (j, 0)),
        out_shape=jax.ShapeDtypeStruct((rows, WIDTH), jnp.bfloat16),
        compiler_params=pltpu.CompilerParams(vmem_limit_bytes=60 * MIB),
        cost_estimate=pl.CostEstimate(
            flops=2 * rows * depth * WIDTH,
            bytes_accessed=2 * depth * (rows + WIDTH),
            transcendentals=0,
        ),
    )(grads, weight, after)


def multiply(turned, g_ref, out_ref):
    parts, owners, share, step = out_ref.shape
    for lo, hi in RANGES:
        wide = dot_nn(turned, g_ref[:, lo:hi])
        for part in range(lo // step, -(-hi // step)):
            first, last = max(lo, part * step), min(hi, (part + 1) * step)
            for block in range(owners):
                piece = wide[block * share : (block + 1) * share, first - lo : last - lo]
                out_ref[part, block, :, first - part * step : last - part * step] = piece.astype(
                    jnp.bfloat16
                )
    tail = 3 * WIDTH - (parts - 1) * step
    out_ref[parts - 1, :, :, tail:] = jnp.zeros((owners, share, step - tail), jnp.bfloat16)


def sent_kernel(
    core_ref, x_hbm, g_ref, out_ref, own_ref, x_scr, wide_scr, turned_scr, x_sems
):
    chunks, rows = x_scr.shape[:2]
    share = out_ref.shape[2]
    x_copies = [
        pltpu.make_async_copy(x_hbm.at[pl.ds(i * rows, rows), :], x_scr.at[i], x_sems.at[i])
        for i in range(chunks)
    ]
    for copy in x_copies:
        copy.start()
    for i, copy in enumerate(x_copies):
        copy.wait()
        flipped = x_scr[i].astype(jnp.float32).T
        for n, turned_ref in enumerate((own_ref, turned_scr)):
            for block in range(out_ref.shape[1]):
                lo = 2 * block * share
                even, odd = flipped[lo : lo + share], flipped[lo + share : lo + 2 * share]
                wide_scr[n, block * share : (block + 1) * share, :] = jnp.where(
                    core_ref[0] == n, even, odd
                )
            turned_ref[:, i * rows : (i + 1) * rows] = wide_scr[n].astype(jnp.bfloat16)
    multiply(turned_scr[...], g_ref, out_ref)


def own_kernel(turned_ref, g_ref, out_ref):
    multiply(turned_ref[...], g_ref, out_ref)


def weight_grad_sent(core, tokens, grads, parts, step, owners):
    rows, chunks = tokens.shape[0], 4
    half = WIDTH // 2
    vmem = pl.BlockSpec(memory_space=pltpu.VMEM)
    hbm = pl.BlockSpec(memory_space=pltpu.HBM)
    return pl.pallas_call(
        sent_kernel,
        in_specs=[pl.BlockSpec(memory_space=pltpu.SMEM), hbm, vmem],
        out_specs=[vmem, vmem],
        out_shape=[
            jax.ShapeDtypeStruct((parts, owners, half // owners, step), jnp.bfloat16),
            jax.ShapeDtypeStruct((half, rows), jnp.bfloat16),
        ],
        scratch_shapes=[
            pltpu.VMEM((chunks, rows // chunks, WIDTH), jnp.bfloat16),
            pltpu.VMEM((2, half, rows // chunks), jnp.float32),
            pltpu.VMEM((half, rows), jnp.bfloat16),
            pltpu.SemaphoreType.DMA((chunks,)),
        ],
        compiler_params=pltpu.CompilerParams(vmem_limit_bytes=36 * MIB),
        cost_estimate=pl.CostEstimate(
            flops=rows * WIDTH * step * parts,
            bytes_accessed=rows * (2 * WIDTH + 2 * step * parts) + WIDTH * step * parts,
            transcendentals=0,
        ),
    )(core, tokens, grads)


def weight_grad_own(turned, grads, parts, step, owners):
    half, rows = turned.shape
    vmem = pl.BlockSpec(memory_space=pltpu.VMEM)
    return pl.pallas_call(
        own_kernel,
        in_specs=[vmem, vmem],
        out_specs=vmem,
        out_shape=jax.ShapeDtypeStruct((parts, owners, half // owners, step), jnp.bfloat16),
        compiler_params=pltpu.CompilerParams(vmem_limit_bytes=36 * MIB),
        cost_estimate=pl.CostEstimate(
            flops=rows * WIDTH * step * parts,
            bytes_accessed=rows * (WIDTH + 2 * step * parts) + WIDTH * step * parts,
            transcendentals=0,
        ),
    )(turned, grads)


def swap(value, axis):
    return lax.ppermute(value, axis, [(0, 1), (1, 0)])


def add(first, second):
    return (first.astype(jnp.float32) + second.astype(jnp.float32)).astype(jnp.bfloat16)


def fold_kernel(blocks_ref, after_ref, out_ref):
    total = blocks_ref[0].astype(jnp.float32)
    for n in range(1, blocks_ref.shape[0]):
        total = total + blocks_ref[n].astype(jnp.float32)
    out_ref[...] = total.astype(jnp.bfloat16)


def fold(blocks, after):
    vmem = pl.BlockSpec(memory_space=pltpu.VMEM)
    return pl.pallas_call(
        fold_kernel,
        in_specs=[vmem, pl.BlockSpec(memory_space=pl.ANY)],
        out_specs=vmem,
        out_shape=jax.ShapeDtypeStruct(blocks.shape[1:], jnp.bfloat16),
        compiler_params=pltpu.CompilerParams(vmem_limit_bytes=16 * MIB),
        cost_estimate=pl.CostEstimate(
            flops=blocks.size, bytes_accessed=2 * blocks.size, transcendentals=0
        ),
    )(blocks, after)


def join_kernel(scale, z_ref, *refs):
    out_ref = refs[-1]
    parts = len(refs) - 1
    step = refs[0].shape[1]
    whole = out_ref.shape[1] - (parts - 1) * step
    for n, ref in enumerate(refs[:-1]):
        part = z_ref[0] ^ n
        lo = pl.multiple_of(part * step, LANES)
        out_ref[:, pl.ds(lo, whole)] = ref[:, :whole].astype(jnp.float32) * scale

        @pl.when(part < parts - 1)
        def _():
            rest = pl.multiple_of(part * step + whole, LANES)
            out_ref[:, pl.ds(rest, step - whole)] = ref[:, whole:].astype(jnp.float32) * scale


def join(z, blocks, scale):
    vmem = pl.BlockSpec(memory_space=pltpu.VMEM)
    rows = blocks[0].shape[0]
    return pl.pallas_call(
        functools.partial(join_kernel, scale),
        in_specs=[pl.BlockSpec(memory_space=pltpu.SMEM)] + [vmem] * len(blocks),
        out_specs=vmem,
        out_shape=jax.ShapeDtypeStruct((rows, 3 * WIDTH), jnp.float32),
        compiler_params=pltpu.CompilerParams(vmem_limit_bytes=16 * MIB),
        cost_estimate=pl.CostEstimate(
            flops=rows * 3 * WIDTH, bytes_accessed=6 * rows * 3 * WIDTH, transcendentals=0
        ),
    )(z, *blocks)


def per_device(layer_input, queries, keys, values, d_attn, w_qkv):
    devices = lax.axis_size(SEQ)
    parts = lax.axis_size("z")
    owners = devices // lax.axis_size("core")
    clips = parts * lax.axis_size("xh")
    frames, spatial = layer_input.shape[1], layer_input.shape[2]
    cells = spatial // devices
    rows = devices * frames * cells
    norm_scale = 1.0 / math.sqrt(clips * FRAMES * SPATIAL)
    core = lax.axis_index("core").reshape(1).astype(jnp.int32)

    sent = pack([queries, keys, values, d_attn], devices)
    received = lax.all_to_all(sent, SEQ, 0, 0, tiled=True)
    sent_x = pack([layer_input], devices)
    tokens = lax.all_to_all(sent_x, SEQ, 0, 0, tiled=True).reshape(rows, WIDTH)

    grads = attend(received)
    step = -(-3 * WIDTH // (parts * LANES)) * LANES
    sent_part, turned = weight_grad_sent(core, tokens, grads, parts, step, owners)
    own_part = weight_grad_own(turned, grads, parts, step, owners)
    kept = add(own_part, swap(sent_part, "core"))
    over_z = lax.psum_scatter(kept, "z", scatter_dimension=0, tiled=True)[0]

    d_local = input_grad(grads, w_qkv, kept).reshape(devices, frames, cells, WIDTH)
    d_input = unpack(lax.all_to_all(d_local, SEQ, 0, 0, tiled=True))

    share = fold(lax.all_to_all(over_z, ("y", "xl"), 0, 0, tiled=True), d_input)
    share = add(share, swap(share, "xh"))
    blocks = [share] + [
        lax.ppermute(share, "z", [(i, i ^ n) for i in range(parts)]) for n in range(1, parts)
    ]
    d_weight = join(lax.axis_index("z").reshape(1).astype(jnp.int32), blocks, norm_scale)
    return (d_input, d_weight)


def solution(mesh):
    sizes = (4, 2, 4, 2, 2)
    fine = Mesh(mesh.devices.reshape(sizes), ("z", "xh", "y", "xl", "core"))
    dp = ("z", "xh")
    block = P(dp, SEQ, None, None)
    return jax.shard_map(
        per_device,
        mesh=fine,
        in_specs=(block,) * 5 + (P(),),
        out_specs=(block, P(SEQ, None)),
        check_vma=False,
    )
```

```python
import functools
import math

import jax
import jax.numpy as jnp
from jax import lax
from jax.experimental import pallas as pl
from jax.experimental.pallas import tpu as pltpu
from jax.sharding import Mesh
from jax.sharding import PartitionSpec as P

HEADS = 16
HEAD_DIM = 72
FRAMES = 64
SPATIAL = 256
WIDTH = HEADS * HEAD_DIM
LANES = 128
TILES = WIDTH // LANES
FACTOR = HEAD_DIM ** (-0.5)
SEQ = ("y", "xl", "core")
EARLY_ROWS = 256
SPLIT = 1792
MIB = 1024 * 1024


def pack_kernel(cells, group, *refs):
    out_ref = refs[-1]
    for n, ref in enumerate(refs[:-1]):
        for i in range(group):
            out_ref[i, n] = ref[0, :, i * cells : (i + 1) * cells, :]


def pack(arrays, devices):
    frames, cells = arrays[0].shape[1], arrays[0].shape[2] // devices
    group = 4
    block = pl.BlockSpec((1, frames, group * cells, WIDTH), lambda j: (0, 0, j, 0))
    count = len(arrays)
    return pl.pallas_call(
        functools.partial(pack_kernel, cells, group),
        grid=(devices // group,),
        in_specs=[block] * count,
        out_specs=pl.BlockSpec((group, count, frames, cells, WIDTH), lambda j: (j, 0, 0, 0, 0)),
        out_shape=jax.ShapeDtypeStruct((devices, count, frames, cells, WIDTH), jnp.bfloat16),
        compiler_params=pltpu.CompilerParams(vmem_limit_bytes=60 * MIB),
        cost_estimate=pl.CostEstimate(
            flops=0, bytes_accessed=2 * count * arrays[0].size * 2, transcendentals=0
        ),
    )(*arrays)


def unpack_kernel(cells, group, in_ref, out_ref):
    for i in range(group):
        out_ref[0, :, i * cells : (i + 1) * cells, :] = in_ref[i]


def unpack(blocks):
    devices, frames, cells, width = blocks.shape
    group = 4
    return pl.pallas_call(
        functools.partial(unpack_kernel, cells, group),
        grid=(devices // group,),
        in_specs=[pl.BlockSpec((group, frames, cells, width), lambda j: (j, 0, 0, 0))],
        out_specs=pl.BlockSpec((1, frames, group * cells, width), lambda j: (0, 0, j, 0)),
        out_shape=jax.ShapeDtypeStruct((1, frames, cells * devices, width), jnp.bfloat16),
        compiler_params=pltpu.CompilerParams(vmem_limit_bytes=60 * MIB),
        cost_estimate=pl.CostEstimate(flops=0, bytes_accessed=4 * blocks.size, transcendentals=0),
    )(blocks)


def dot_nt(a, b):
    return lax.dot_general(a, b, (((1,), (1,)), ((), ())), preferred_element_type=jnp.float32)


def dot_tn(a, b):
    return lax.dot_general(a, b, (((0,), (0,)), ((), ())), preferred_element_type=jnp.float32)


def dot_nn(a, b):
    return jnp.dot(a, b, preferred_element_type=jnp.float32)


def attend_kernel(
    cells, r_ref, w_hbm, g0_ref, g1_ref, i_hbm, q_scr, k_scr, v_scr, d_scr, w_scr, i_scr, w_sem, i_sem
):
    w_copy = pltpu.make_async_copy(w_hbm, w_scr, w_sem)
    w_copy.start()
    rows = FRAMES * cells
    scratches = (q_scr, k_scr, v_scr, d_scr)
    for n, scr in enumerate(scratches):
        for t in range(TILES):
            tile = r_ref[:, n, :, :, t * LANES : (t + 1) * LANES]
            scr[t] = tile.reshape(rows, LANES).astype(jnp.float32)

    pair_rows = 2 * FRAMES
    lane = lax.broadcasted_iota(jnp.int32, (FRAMES, 2 * pair_rows), 1)
    left = lane % pair_rows < FRAMES

    def compact(block):
        return jnp.where(left, block[:FRAMES], block[FRAMES:])

    def spread(block):
        zero = jnp.zeros_like(block)
        upper = jnp.where(left, block, zero)
        lower = jnp.where(left, zero, block)
        return jnp.concatenate([upper, lower], axis=0).astype(jnp.bfloat16)

    def pair_step(i, carry):
        p = 2 * i

        def load(scr, t):
            first = scr[t, pl.ds(p, FRAMES, stride=cells), :]
            second = scr[t, pl.ds(p + 1, FRAMES, stride=cells), :]
            return jnp.concatenate([first, second], axis=0).astype(jnp.bfloat16)

        q_t, k_t, v_t, d_t = ([load(scr, t) for t in range(TILES)] for scr in scratches)
        acc = [dict(), dict(), dict()]

        def put(n, t, value):
            acc[n][t] = acc[n][t] + value if t in acc[n] else value

        def scores(h):
            start = h * HEAD_DIM
            first = start // LANES
            low = start - first * LANES
            window_lane = lax.broadcasted_iota(jnp.int32, (1, 2 * LANES), 1)
            masks = [
                ((window_lane >= lo) & (window_lane < lo + HEAD_DIM)).astype(jnp.bfloat16)
                for lo in (low, low + HEAD_DIM)
            ]

            def window(parts):
                return jnp.concatenate([parts[first], parts[first + 1]], axis=1)

            def both(value):
                return jnp.concatenate([value * mask for mask in masks], axis=0)

            k_w = window(k_t)
            q_h = both(window(q_t))
            d_h = both(window(d_t))
            raw = compact(dot_nt(k_w, q_h))
            grad_p = compact(dot_nt(window(v_t), d_h))
            return k_w, q_h, d_h, raw, grad_p

        def soft(k_w, q_h, d_h, raw, grad_p):
            exp_term = jnp.exp((raw - jnp.max(raw, axis=0, keepdims=True)) * FACTOR)
            prob = exp_term * (1.0 / jnp.sum(exp_term, axis=0, keepdims=True))
            prob_low = prob.astype(jnp.bfloat16).astype(jnp.float32)
            delta = jnp.sum(prob_low * grad_p, axis=0, keepdims=True)
            grad_s = spread(prob * (grad_p - delta))
            return k_w, q_h, d_h, spread(prob), grad_s

        def grads(h, k_w, q_h, d_h, prob_low, grad_s):
            start = h * HEAD_DIM
            first = start // LANES
            low = start - first * LANES
            window_lane = lax.broadcasted_iota(jnp.int32, (1, 2 * LANES), 1)
            own = (window_lane >= low) & (window_lane < low + 2 * HEAD_DIM)
            from_keys = dot_tn(grad_s, k_w)
            halves = jnp.where(
                window_lane < low + HEAD_DIM, from_keys[:pair_rows], from_keys[pair_rows:]
            )
            results = (
                jnp.where(own, halves, 0.0),
                dot_nn(grad_s, q_h),
                dot_nn(prob_low, d_h),
            )
            for n, result in enumerate(results):
                put(n, first, result[:, :LANES])
                put(n, first + 1, result[:, LANES:])
            for t in range(first, (start + 2 * HEAD_DIM) // LANES):
                for n, scr in enumerate((q_scr, k_scr, v_scr)):
                    value = acc[n].pop(t)
                    scr[t, pl.ds(p, FRAMES, stride=cells), :] = value[:FRAMES]
                    scr[t, pl.ds(p + 1, FRAMES, stride=cells), :] = value[FRAMES:]

        steps = HEADS // 2
        scored, softened = {}, {}
        for at in range(steps + 2):
            if at < steps:
                scored[at] = scores(2 * at)
            if at >= 2:
                grads(2 * (at - 2), *softened.pop(at - 2))
            if 1 <= at <= steps:
                softened[at - 1] = soft(*scored.pop(at - 1))
        return carry

    lax.fori_loop(0, cells // 2, pair_step, 0)
    for n, scr in enumerate((q_scr, k_scr, v_scr)):
        for t in range(TILES):
            lo = n * WIDTH + t * LANES
            scale = 1.0 if n == 2 else FACTOR
            g_ref, lo = (g0_ref, lo) if lo < SPLIT else (g1_ref, lo - SPLIT)
            g_ref[:, lo : lo + LANES] = (scr[t] * scale).astype(jnp.bfloat16)
    w_copy.wait()
    i_scr[...] = (
        dot_nt(g0_ref[:EARLY_ROWS, :], w_scr[:, :SPLIT])
        + dot_nt(g1_ref[:EARLY_ROWS, :], w_scr[:, SPLIT:])
    ).astype(jnp.bfloat16)
    i_copy = pltpu.make_async_copy(i_scr, i_hbm.at[pl.ds(0, EARLY_ROWS), :], i_sem)
    i_copy.start()
    i_copy.wait()


def attend(received, weight):
    devices, _, frames, cells, _ = received.shape
    rows = devices * frames * cells
    scratch = pltpu.VMEM((TILES, rows, LANES), jnp.float32)
    vmem = pl.BlockSpec(memory_space=pltpu.VMEM)
    return pl.pallas_call(
        functools.partial(attend_kernel, cells),
        in_specs=[vmem, pl.BlockSpec(memory_space=pl.ANY)],
        out_specs=[vmem, vmem, pl.BlockSpec(memory_space=pltpu.HBM)],
        out_shape=[
            jax.ShapeDtypeStruct((rows, SPLIT), jnp.bfloat16),
            jax.ShapeDtypeStruct((rows, 3 * WIDTH - SPLIT), jnp.bfloat16),
            jax.ShapeDtypeStruct((rows, WIDTH), jnp.bfloat16),
        ],
        scratch_shapes=[scratch] * 4
        + [
            pltpu.VMEM(weight.shape, jnp.bfloat16),
            pltpu.VMEM((EARLY_ROWS, WIDTH), jnp.bfloat16),
            pltpu.SemaphoreType.DMA,
            pltpu.SemaphoreType.DMA,
        ],
        compiler_params=pltpu.CompilerParams(vmem_limit_bytes=60 * MIB),
        cost_estimate=pl.CostEstimate(
            flops=24_000_000_000, bytes_accessed=14 * rows * WIDTH, transcendentals=4_000_000
        ),
    )(received, weight)


def input_grad_kernel(g0_ref, g1_ref, w_ref, early_ref, after_ref, out_ref):
    out_ref[...] = (
        dot_nt(g0_ref[...], w_ref[:, :SPLIT]) + dot_nt(g1_ref[...], w_ref[:, SPLIT:])
    ).astype(jnp.bfloat16)


def input_grad(grads, weight, early, after):
    rows, depth = early.shape[0], weight.shape[1]
    step = EARLY_ROWS
    return pl.pallas_call(
        input_grad_kernel,
        grid=(rows // step - 1,),
        in_specs=[
            pl.BlockSpec((step, SPLIT), lambda j: (j + 1, 0)),
            pl.BlockSpec((step, depth - SPLIT), lambda j: (j + 1, 0)),
            pl.BlockSpec((WIDTH, depth), lambda j: (0, 0)),
            pl.BlockSpec(memory_space=pl.ANY),
            pl.BlockSpec(memory_space=pl.ANY),
        ],
        out_specs=pl.BlockSpec((step, WIDTH), lambda j: (j + 1, 0)),
        out_shape=jax.ShapeDtypeStruct((rows, WIDTH), jnp.bfloat16),
        input_output_aliases={3: 0},
        compiler_params=pltpu.CompilerParams(vmem_limit_bytes=60 * MIB),
        cost_estimate=pl.CostEstimate(
            flops=2 * rows * depth * WIDTH,
            bytes_accessed=2 * depth * (rows + WIDTH),
            transcendentals=0,
        ),
    )(*grads, weight, early, after)


def multiply(turned, g_ref, out_ref, first):
    owners, share, step = out_ref.shape[1:]
    wide = dot_nn(turned, g_ref[...])
    width = wide.shape[1]
    for n in range(-(-width // step)):
        end = min(step, width - n * step)
        for block in range(owners):
            piece = wide[block * share : (block + 1) * share, n * step : n * step + end]
            out_ref[first + n, block, :, :end] = piece.astype(jnp.bfloat16)
        if end < step:
            out_ref[first + n, :, :, end:] = jnp.zeros((owners, share, step - end), jnp.bfloat16)


def turn_kernel(core_ref, x_hbm, g_ref, out_ref, own_ref, sent_ref, x_scr, wide_scr, x_sems):
    chunks, rows = x_scr.shape[:2]
    share = out_ref.shape[2]
    x_copies = [
        pltpu.make_async_copy(x_hbm.at[pl.ds(i * rows, rows), :], x_scr.at[i], x_sems.at[i])
        for i in range(chunks)
    ]
    for copy in x_copies:
        copy.start()
    for i, copy in enumerate(x_copies):
        copy.wait()
        flipped = x_scr[i].astype(jnp.float32).T
        for n, turned_ref in enumerate((own_ref, sent_ref)):
            for block in range(out_ref.shape[1]):
                lo = 2 * block * share
                even, odd = flipped[lo : lo + share], flipped[lo + share : lo + 2 * share]
                wide_scr[n, block * share : (block + 1) * share, :] = jnp.where(
                    core_ref[0] == n, even, odd
                )
            turned_ref[:, i * rows : (i + 1) * rows] = wide_scr[n].astype(jnp.bfloat16)
    multiply(sent_ref[...], g_ref, out_ref, 0)


def product_kernel(turned_ref, *refs):
    out_ref = refs[-1]
    first = 0
    for g_ref in refs[:-1]:
        multiply(turned_ref[...], g_ref, out_ref, first)
        first += g_ref.shape[1] // out_ref.shape[3]


def turn_and_product(core, tokens, grads, parts, step, owners):
    rows, chunks = tokens.shape[0], 4
    half = WIDTH // 2
    vmem = pl.BlockSpec(memory_space=pltpu.VMEM)
    hbm = pl.BlockSpec(memory_space=pltpu.HBM)
    turned = jax.ShapeDtypeStruct((half, rows), jnp.bfloat16)
    return pl.pallas_call(
        turn_kernel,
        in_specs=[pl.BlockSpec(memory_space=pltpu.SMEM), hbm, vmem],
        out_specs=[vmem, vmem, vmem],
        out_shape=[
            jax.ShapeDtypeStruct((parts, owners, half // owners, step), jnp.bfloat16),
            turned,
            turned,
        ],
        scratch_shapes=[
            pltpu.VMEM((chunks, rows // chunks, WIDTH), jnp.bfloat16),
            pltpu.VMEM((2, half, rows // chunks), jnp.float32),
            pltpu.SemaphoreType.DMA((chunks,)),
        ],
        compiler_params=pltpu.CompilerParams(vmem_limit_bytes=36 * MIB),
        cost_estimate=pl.CostEstimate(
            flops=rows * WIDTH * step * parts,
            bytes_accessed=rows * (2 * WIDTH + 2 * step * parts) + WIDTH * step * parts,
            transcendentals=0,
        ),
    )(core, tokens, grads)


def product(turned, ranges, parts, step, owners):
    half, rows = turned.shape
    vmem = pl.BlockSpec(memory_space=pltpu.VMEM)
    return pl.pallas_call(
        product_kernel,
        in_specs=[vmem] * (1 + len(ranges)),
        out_specs=vmem,
        out_shape=jax.ShapeDtypeStruct((parts, owners, half // owners, step), jnp.bfloat16),
        compiler_params=pltpu.CompilerParams(vmem_limit_bytes=36 * MIB),
        cost_estimate=pl.CostEstimate(
            flops=rows * WIDTH * step * parts,
            bytes_accessed=rows * (WIDTH + 2 * step * parts) + WIDTH * step * parts,
            transcendentals=0,
        ),
    )(turned, *ranges)


def add_kernel(own_ref, early_ref, late_ref, out_ref):
    half = pl.num_programs(0) // 2
    at = pl.program_id(0)

    @pl.when(at < half)
    def _():
        out_ref[...] = add(own_ref[...], early_ref[...])

    @pl.when(at >= half)
    def _():
        out_ref[...] = add(own_ref[...], late_ref[...])


def add_parts(own, early, late):
    parts = own.shape[0]
    half = parts // 2
    block = (1,) + own.shape[1:]
    return pl.pallas_call(
        add_kernel,
        grid=(parts,),
        in_specs=[
            pl.BlockSpec(block, lambda j: (j, 0, 0, 0)),
            pl.BlockSpec(block, lambda j: (jnp.minimum(j, half - 1), 0, 0, 0)),
            pl.BlockSpec(block, lambda j: (jnp.maximum(j - half, 0), 0, 0, 0)),
        ],
        out_specs=pl.BlockSpec(block, lambda j: (j, 0, 0, 0)),
        out_shape=jax.ShapeDtypeStruct(own.shape, own.dtype),
        compiler_params=pltpu.CompilerParams(vmem_limit_bytes=36 * MIB),
        cost_estimate=pl.CostEstimate(
            flops=own.size, bytes_accessed=6 * own.size, transcendentals=0
        ),
    )(own, early, late)


def swap(value, axis):
    return lax.ppermute(value, axis, [(0, 1), (1, 0)])


def add(first, second):
    return (first.astype(jnp.float32) + second.astype(jnp.float32)).astype(jnp.bfloat16)


def fold_kernel(blocks_ref, after_ref, out_ref):
    total = blocks_ref[0].astype(jnp.float32)
    for n in range(1, blocks_ref.shape[0]):
        total = total + blocks_ref[n].astype(jnp.float32)
    out_ref[...] = total.astype(jnp.bfloat16)


def fold(blocks, after):
    vmem = pl.BlockSpec(memory_space=pltpu.VMEM)
    return pl.pallas_call(
        fold_kernel,
        in_specs=[vmem, pl.BlockSpec(memory_space=pl.ANY)],
        out_specs=vmem,
        out_shape=jax.ShapeDtypeStruct(blocks.shape[1:], jnp.bfloat16),
        compiler_params=pltpu.CompilerParams(vmem_limit_bytes=16 * MIB),
        cost_estimate=pl.CostEstimate(
            flops=blocks.size, bytes_accessed=2 * blocks.size, transcendentals=0
        ),
    )(blocks, after)


def join_kernel(scale, z_ref, *refs):
    out_ref = refs[-1]
    parts = len(refs) - 1
    step = refs[0].shape[1]
    whole = out_ref.shape[1] - (parts - 1) * step
    for n, ref in enumerate(refs[:-1]):
        part = z_ref[0] ^ n
        lo = pl.multiple_of(part * step, LANES)
        out_ref[:, pl.ds(lo, whole)] = ref[:, :whole].astype(jnp.float32) * scale

        @pl.when(part < parts - 1)
        def _():
            rest = pl.multiple_of(part * step + whole, LANES)
            out_ref[:, pl.ds(rest, step - whole)] = ref[:, whole:].astype(jnp.float32) * scale


def join(z, blocks, scale):
    vmem = pl.BlockSpec(memory_space=pltpu.VMEM)
    rows = blocks[0].shape[0]
    return pl.pallas_call(
        functools.partial(join_kernel, scale),
        in_specs=[pl.BlockSpec(memory_space=pltpu.SMEM)] + [vmem] * len(blocks),
        out_specs=vmem,
        out_shape=jax.ShapeDtypeStruct((rows, 3 * WIDTH), jnp.float32),
        compiler_params=pltpu.CompilerParams(vmem_limit_bytes=16 * MIB),
        cost_estimate=pl.CostEstimate(
            flops=rows * 3 * WIDTH, bytes_accessed=6 * rows * 3 * WIDTH, transcendentals=0
        ),
    )(z, *blocks)


def per_device(layer_input, queries, keys, values, d_attn, w_qkv):
    devices = lax.axis_size(SEQ)
    parts = lax.axis_size("z")
    owners = devices // lax.axis_size("core")
    clips = parts * lax.axis_size("xh")
    frames, spatial = layer_input.shape[1], layer_input.shape[2]
    cells = spatial // devices
    rows = devices * frames * cells
    norm_scale = 1.0 / math.sqrt(clips * FRAMES * SPATIAL)
    core = lax.axis_index("core").reshape(1).astype(jnp.int32)

    sent = pack([queries, keys, values, d_attn], devices)
    received = lax.all_to_all(sent, SEQ, 0, 0, tiled=True)
    sent_x = pack([layer_input], devices)
    tokens = lax.all_to_all(sent_x, SEQ, 0, 0, tiled=True).reshape(rows, WIDTH)

    *grads, early = attend(received, w_qkv)
    step = -(-3 * WIDTH // (parts * LANES)) * LANES
    count = parts // 2
    sent_early, turned_own, turned_sent = turn_and_product(
        core, tokens, grads[0], count, step, owners
    )
    sent_late = product(turned_sent, grads[1:], count, step, owners)
    got_early, got_late = swap(sent_early, "core"), swap(sent_late, "core")
    own_part = product(turned_own, grads, parts, step, owners)
    kept = add_parts(own_part, got_early, got_late)
    over_z = lax.psum_scatter(kept, "z", scatter_dimension=0, tiled=True)[0]

    d_local = input_grad(grads, w_qkv, early, kept).reshape(devices, frames, cells, WIDTH)
    d_input = unpack(lax.all_to_all(d_local, SEQ, 0, 0, tiled=True))

    share = fold(lax.all_to_all(over_z, ("y", "xl"), 0, 0, tiled=True), d_input)
    share = add(share, swap(share, "xh"))
    blocks = [share] + [
        lax.ppermute(share, "z", [(i, i ^ n) for i in range(parts)]) for n in range(1, parts)
    ]
    d_weight = join(lax.axis_index("z").reshape(1).astype(jnp.int32), blocks, norm_scale)
    return (d_input, d_weight)


def solution(mesh):
    sizes = (4, 2, 4, 2, 2)
    fine = Mesh(mesh.devices.reshape(sizes), ("z", "xh", "y", "xl", "core"))
    dp = ("z", "xh")
    block = P(dp, SEQ, None, None)
    return jax.shard_map(
        per_device,
        mesh=fine,
        in_specs=(block,) * 5 + (P(),),
        out_specs=(block, P(SEQ, None)),
        check_vma=False,
    )
```

```python
import functools
import math

import jax
import jax.numpy as jnp
from jax import lax
from jax.experimental import pallas as pl
from jax.experimental.pallas import tpu as pltpu
from jax.sharding import Mesh
from jax.sharding import PartitionSpec as P

HEADS = 16
HEAD_DIM = 72
FRAMES = 64
SPATIAL = 256
WIDTH = HEADS * HEAD_DIM
LANES = 128
TILES = WIDTH // LANES
FACTOR = HEAD_DIM ** (-0.5)
SEQ = ("y", "xl", "core")
EARLY_ROWS = 256
SPLIT = 1792
MIB = 1024 * 1024


def pack_kernel(cells, group, *refs):
    out_ref = refs[-1]
    for n, ref in enumerate(refs[:-1]):
        for i in range(group):
            out_ref[i, n] = ref[0, :, i * cells : (i + 1) * cells, :]


def pack(arrays, devices):
    frames, cells = arrays[0].shape[1], arrays[0].shape[2] // devices
    group = 8
    block = pl.BlockSpec((1, frames, group * cells, WIDTH), lambda j: (0, 0, j, 0))
    count = len(arrays)
    return pl.pallas_call(
        functools.partial(pack_kernel, cells, group),
        grid=(devices // group,),
        in_specs=[block] * count,
        out_specs=pl.BlockSpec((group, count, frames, cells, WIDTH), lambda j: (j, 0, 0, 0, 0)),
        out_shape=jax.ShapeDtypeStruct((devices, count, frames, cells, WIDTH), jnp.bfloat16),
        compiler_params=pltpu.CompilerParams(vmem_limit_bytes=60 * MIB),
        cost_estimate=pl.CostEstimate(
            flops=0, bytes_accessed=2 * count * arrays[0].size * 2, transcendentals=0
        ),
    )(*arrays)


def unpack_kernel(cells, group, in_ref, out_ref):
    for i in range(group):
        out_ref[0, :, i * cells : (i + 1) * cells, :] = in_ref[i]


def unpack(blocks):
    devices, frames, cells, width = blocks.shape
    group = 4
    return pl.pallas_call(
        functools.partial(unpack_kernel, cells, group),
        grid=(devices // group,),
        in_specs=[pl.BlockSpec((group, frames, cells, width), lambda j: (j, 0, 0, 0))],
        out_specs=pl.BlockSpec((1, frames, group * cells, width), lambda j: (0, 0, j, 0)),
        out_shape=jax.ShapeDtypeStruct((1, frames, cells * devices, width), jnp.bfloat16),
        compiler_params=pltpu.CompilerParams(vmem_limit_bytes=60 * MIB),
        cost_estimate=pl.CostEstimate(flops=0, bytes_accessed=4 * blocks.size, transcendentals=0),
    )(blocks)


def dot_nt(a, b):
    return lax.dot_general(a, b, (((1,), (1,)), ((), ())), preferred_element_type=jnp.float32)


def dot_tn(a, b):
    return lax.dot_general(a, b, (((0,), (0,)), ((), ())), preferred_element_type=jnp.float32)


def dot_nn(a, b):
    return jnp.dot(a, b, preferred_element_type=jnp.float32)


def attend_kernel(
    cells, r_ref, w_hbm, g0_ref, g1_ref, i_hbm, q_scr, k_scr, v_scr, d_scr, w_scr, i_scr, w_sem, i_sem
):
    w_copy = pltpu.make_async_copy(w_hbm, w_scr, w_sem)
    w_copy.start()
    rows = FRAMES * cells
    scratches = (q_scr, k_scr, v_scr, d_scr)
    for n, scr in enumerate(scratches):
        for t in range(TILES):
            tile = r_ref[:, n, :, :, t * LANES : (t + 1) * LANES]
            scr[t] = tile.reshape(rows, LANES).astype(jnp.float32)

    pair_rows = 2 * FRAMES
    lane = lax.broadcasted_iota(jnp.int32, (FRAMES, 2 * pair_rows), 1)
    left = lane % pair_rows < FRAMES

    def compact(block):
        return jnp.where(left, block[:FRAMES], block[FRAMES:])

    def spread(block):
        zero = jnp.zeros_like(block)
        upper = jnp.where(left, block, zero)
        lower = jnp.where(left, zero, block)
        return jnp.concatenate([upper, lower], axis=0).astype(jnp.bfloat16)

    def pair_step(i, carry):
        p = 2 * i

        def load(scr, t):
            first = scr[t, pl.ds(p, FRAMES, stride=cells), :]
            second = scr[t, pl.ds(p + 1, FRAMES, stride=cells), :]
            return jnp.concatenate([first, second], axis=0).astype(jnp.bfloat16)

        q_t, k_t, v_t, d_t = ([load(scr, t) for t in range(TILES)] for scr in scratches)
        acc = [dict(), dict(), dict()]

        def put(n, t, value):
            acc[n][t] = acc[n][t] + value if t in acc[n] else value

        def scores(h):
            start = h * HEAD_DIM
            first = start // LANES
            low = start - first * LANES
            window_lane = lax.broadcasted_iota(jnp.int32, (1, 2 * LANES), 1)
            masks = [
                ((window_lane >= lo) & (window_lane < lo + HEAD_DIM)).astype(jnp.bfloat16)
                for lo in (low, low + HEAD_DIM)
            ]

            def window(parts):
                return jnp.concatenate([parts[first], parts[first + 1]], axis=1)

            def both(value):
                return jnp.concatenate([value * mask for mask in masks], axis=0)

            k_w = window(k_t)
            q_h = both(window(q_t))
            d_h = both(window(d_t))
            raw = compact(dot_nt(k_w, q_h))
            grad_p = compact(dot_nt(window(v_t), d_h))
            return k_w, q_h, d_h, raw, grad_p

        def soft(k_w, q_h, d_h, raw, grad_p):
            exp_term = jnp.exp((raw - jnp.max(raw, axis=0, keepdims=True)) * FACTOR)
            prob = exp_term * (1.0 / jnp.sum(exp_term, axis=0, keepdims=True))
            prob_low = prob.astype(jnp.bfloat16).astype(jnp.float32)
            delta = jnp.sum(prob_low * grad_p, axis=0, keepdims=True)
            grad_s = spread(prob * (grad_p - delta))
            return k_w, q_h, d_h, spread(prob), grad_s

        def grads(h, k_w, q_h, d_h, prob_low, grad_s):
            start = h * HEAD_DIM
            first = start // LANES
            low = start - first * LANES
            window_lane = lax.broadcasted_iota(jnp.int32, (1, 2 * LANES), 1)
            own = (window_lane >= low) & (window_lane < low + 2 * HEAD_DIM)
            from_keys = dot_tn(grad_s, k_w)
            halves = jnp.where(
                window_lane < low + HEAD_DIM, from_keys[:pair_rows], from_keys[pair_rows:]
            )
            results = (
                jnp.where(own, halves, 0.0),
                dot_nn(grad_s, q_h),
                dot_nn(prob_low, d_h),
            )
            for n, result in enumerate(results):
                put(n, first, result[:, :LANES])
                put(n, first + 1, result[:, LANES:])
            for t in range(first, (start + 2 * HEAD_DIM) // LANES):
                for n, scr in enumerate((q_scr, k_scr, v_scr)):
                    value = acc[n].pop(t)
                    scr[t, pl.ds(p, FRAMES, stride=cells), :] = value[:FRAMES]
                    scr[t, pl.ds(p + 1, FRAMES, stride=cells), :] = value[FRAMES:]

        steps = HEADS // 2
        scored, softened = {}, {}
        for at in range(steps + 2):
            if at < steps:
                scored[at] = scores(2 * at)
            if at >= 2:
                grads(2 * (at - 2), *softened.pop(at - 2))
            if 1 <= at <= steps:
                softened[at - 1] = soft(*scored.pop(at - 1))
        return carry

    lax.fori_loop(0, cells // 2, pair_step, 0)
    for n, scr in enumerate((q_scr, k_scr, v_scr)):
        for t in range(TILES):
            lo = n * WIDTH + t * LANES
            scale = 1.0 if n == 2 else FACTOR
            g_ref, lo = (g0_ref, lo) if lo < SPLIT else (g1_ref, lo - SPLIT)
            g_ref[:, lo : lo + LANES] = (scr[t] * scale).astype(jnp.bfloat16)
    w_copy.wait()
    i_scr[...] = (
        dot_nt(g0_ref[:EARLY_ROWS, :], w_scr[:, :SPLIT])
        + dot_nt(g1_ref[:EARLY_ROWS, :], w_scr[:, SPLIT:])
    ).astype(jnp.bfloat16)
    i_copy = pltpu.make_async_copy(i_scr, i_hbm.at[pl.ds(0, EARLY_ROWS), :], i_sem)
    i_copy.start()
    i_copy.wait()


def attend(received, weight):
    devices, _, frames, cells, _ = received.shape
    rows = devices * frames * cells
    scratch = pltpu.VMEM((TILES, rows, LANES), jnp.float32)
    vmem = pl.BlockSpec(memory_space=pltpu.VMEM)
    return pl.pallas_call(
        functools.partial(attend_kernel, cells),
        in_specs=[vmem, pl.BlockSpec(memory_space=pl.ANY)],
        out_specs=[vmem, vmem, pl.BlockSpec(memory_space=pltpu.HBM)],
        out_shape=[
            jax.ShapeDtypeStruct((rows, SPLIT), jnp.bfloat16),
            jax.ShapeDtypeStruct((rows, 3 * WIDTH - SPLIT), jnp.bfloat16),
            jax.ShapeDtypeStruct((rows, WIDTH), jnp.bfloat16),
        ],
        scratch_shapes=[scratch] * 4
        + [
            pltpu.VMEM(weight.shape, jnp.bfloat16),
            pltpu.VMEM((EARLY_ROWS, WIDTH), jnp.bfloat16),
            pltpu.SemaphoreType.DMA,
            pltpu.SemaphoreType.DMA,
        ],
        compiler_params=pltpu.CompilerParams(vmem_limit_bytes=60 * MIB),
        cost_estimate=pl.CostEstimate(
            flops=24_000_000_000, bytes_accessed=14 * rows * WIDTH, transcendentals=4_000_000
        ),
    )(received, weight)


def input_grad_kernel(g0_ref, g1_ref, w_ref, early_ref, after_ref, out_ref):
    out_ref[...] = (
        dot_nt(g0_ref[...], w_ref[:, :SPLIT]) + dot_nt(g1_ref[...], w_ref[:, SPLIT:])
    ).astype(jnp.bfloat16)


def input_grad(grads, weight, early, after):
    rows, depth = early.shape[0], weight.shape[1]
    step = EARLY_ROWS
    return pl.pallas_call(
        input_grad_kernel,
        grid=(rows // step - 1,),
        in_specs=[
            pl.BlockSpec((step, SPLIT), lambda j: (j + 1, 0)),
            pl.BlockSpec((step, depth - SPLIT), lambda j: (j + 1, 0)),
            pl.BlockSpec((WIDTH, depth), lambda j: (0, 0)),
            pl.BlockSpec(memory_space=pl.ANY),
            pl.BlockSpec(memory_space=pl.ANY),
        ],
        out_specs=pl.BlockSpec((step, WIDTH), lambda j: (j + 1, 0)),
        out_shape=jax.ShapeDtypeStruct((rows, WIDTH), jnp.bfloat16),
        input_output_aliases={3: 0},
        compiler_params=pltpu.CompilerParams(vmem_limit_bytes=60 * MIB),
        cost_estimate=pl.CostEstimate(
            flops=2 * rows * depth * WIDTH,
            bytes_accessed=2 * depth * (rows + WIDTH),
            transcendentals=0,
        ),
    )(*grads, weight, early, after)


def multiply(turned, g_ref, out_ref, first):
    owners, share, step = out_ref.shape[1:]
    wide = dot_nn(turned, g_ref[...])
    width = wide.shape[1]
    for n in range(-(-width // step)):
        end = min(step, width - n * step)
        for block in range(owners):
            piece = wide[block * share : (block + 1) * share, n * step : n * step + end]
            out_ref[first + n, block, :, :end] = piece.astype(jnp.bfloat16)
        if end < step:
            out_ref[first + n, :, :, end:] = jnp.zeros((owners, share, step - end), jnp.bfloat16)


def turn_kernel(core_ref, x_hbm, g_ref, out_ref, own_ref, sent_ref, x_scr, wide_scr, x_sems):
    chunks, rows = x_scr.shape[:2]
    share = out_ref.shape[2]
    x_copies = [
        pltpu.make_async_copy(x_hbm.at[pl.ds(i * rows, rows), :], x_scr.at[i], x_sems.at[i])
        for i in range(chunks)
    ]
    for copy in x_copies:
        copy.start()
    for i, copy in enumerate(x_copies):
        copy.wait()
        flipped = x_scr[i].astype(jnp.float32).T
        for n, turned_ref in enumerate((own_ref, sent_ref)):
            for block in range(out_ref.shape[1]):
                lo = 2 * block * share
                even, odd = flipped[lo : lo + share], flipped[lo + share : lo + 2 * share]
                wide_scr[n, block * share : (block + 1) * share, :] = jnp.where(
                    core_ref[0] == n, even, odd
                )
            turned_ref[:, i * rows : (i + 1) * rows] = wide_scr[n].astype(jnp.bfloat16)
    multiply(sent_ref[...], g_ref, out_ref, 0)


def product_kernel(turned_ref, *refs):
    out_ref = refs[-1]
    first = 0
    for g_ref in refs[:-1]:
        multiply(turned_ref[...], g_ref, out_ref, first)
        first += g_ref.shape[1] // out_ref.shape[3]


def turn_and_product(core, tokens, grads, parts, step, owners):
    rows, chunks = tokens.shape[0], 4
    half = WIDTH // 2
    vmem = pl.BlockSpec(memory_space=pltpu.VMEM)
    hbm = pl.BlockSpec(memory_space=pltpu.HBM)
    turned = jax.ShapeDtypeStruct((half, rows), jnp.bfloat16)
    return pl.pallas_call(
        turn_kernel,
        in_specs=[pl.BlockSpec(memory_space=pltpu.SMEM), hbm, vmem],
        out_specs=[vmem, vmem, vmem],
        out_shape=[
            jax.ShapeDtypeStruct((parts, owners, half // owners, step), jnp.bfloat16),
            turned,
            turned,
        ],
        scratch_shapes=[
            pltpu.VMEM((chunks, rows // chunks, WIDTH), jnp.bfloat16),
            pltpu.VMEM((2, half, rows // chunks), jnp.float32),
            pltpu.SemaphoreType.DMA((chunks,)),
        ],
        compiler_params=pltpu.CompilerParams(vmem_limit_bytes=36 * MIB),
        cost_estimate=pl.CostEstimate(
            flops=rows * WIDTH * step * parts,
            bytes_accessed=rows * (2 * WIDTH + 2 * step * parts) + WIDTH * step * parts,
            transcendentals=0,
        ),
    )(core, tokens, grads)


def product(turned, ranges, parts, step, owners):
    half, rows = turned.shape
    vmem = pl.BlockSpec(memory_space=pltpu.VMEM)
    return pl.pallas_call(
        product_kernel,
        in_specs=[vmem] * (1 + len(ranges)),
        out_specs=vmem,
        out_shape=jax.ShapeDtypeStruct((parts, owners, half // owners, step), jnp.bfloat16),
        compiler_params=pltpu.CompilerParams(vmem_limit_bytes=36 * MIB),
        cost_estimate=pl.CostEstimate(
            flops=rows * WIDTH * step * parts,
            bytes_accessed=rows * (WIDTH + 2 * step * parts) + WIDTH * step * parts,
            transcendentals=0,
        ),
    )(turned, *ranges)


def add_kernel(own_ref, early_ref, late_ref, out_ref):
    half = pl.num_programs(0) // 2
    at = pl.program_id(0)

    @pl.when(at < half)
    def _():
        out_ref[...] = add(own_ref[...], early_ref[...])

    @pl.when(at >= half)
    def _():
        out_ref[...] = add(own_ref[...], late_ref[...])


def add_parts(own, early, late):
    parts = own.shape[0]
    half = parts // 2
    block = (1,) + own.shape[1:]
    return pl.pallas_call(
        add_kernel,
        grid=(parts,),
        in_specs=[
            pl.BlockSpec(block, lambda j: (j, 0, 0, 0)),
            pl.BlockSpec(block, lambda j: (jnp.minimum(j, half - 1), 0, 0, 0)),
            pl.BlockSpec(block, lambda j: (jnp.maximum(j - half, 0), 0, 0, 0)),
        ],
        out_specs=pl.BlockSpec(block, lambda j: (j, 0, 0, 0)),
        out_shape=jax.ShapeDtypeStruct(own.shape, own.dtype),
        compiler_params=pltpu.CompilerParams(vmem_limit_bytes=36 * MIB),
        cost_estimate=pl.CostEstimate(
            flops=own.size, bytes_accessed=6 * own.size, transcendentals=0
        ),
    )(own, early, late)


def swap(value, axis):
    return lax.ppermute(value, axis, [(0, 1), (1, 0)])


def add(first, second):
    return (first.astype(jnp.float32) + second.astype(jnp.float32)).astype(jnp.bfloat16)


def fold_kernel(blocks_ref, after_ref, out_ref):
    total = blocks_ref[0].astype(jnp.float32)
    for n in range(1, blocks_ref.shape[0]):
        total = total + blocks_ref[n].astype(jnp.float32)
    out_ref[...] = total.astype(jnp.bfloat16)


def fold(blocks, after):
    vmem = pl.BlockSpec(memory_space=pltpu.VMEM)
    return pl.pallas_call(
        fold_kernel,
        in_specs=[vmem, pl.BlockSpec(memory_space=pl.ANY)],
        out_specs=vmem,
        out_shape=jax.ShapeDtypeStruct(blocks.shape[1:], jnp.bfloat16),
        compiler_params=pltpu.CompilerParams(vmem_limit_bytes=16 * MIB),
        cost_estimate=pl.CostEstimate(
            flops=blocks.size, bytes_accessed=2 * blocks.size, transcendentals=0
        ),
    )(blocks, after)


def join_kernel(scale, z_ref, *refs):
    out_ref = refs[-1]
    parts = len(refs) - 1
    step = refs[0].shape[1]
    whole = out_ref.shape[1] - (parts - 1) * step
    for n, ref in enumerate(refs[:-1]):
        part = z_ref[0] ^ n
        lo = pl.multiple_of(part * step, LANES)
        out_ref[:, pl.ds(lo, whole)] = ref[:, :whole].astype(jnp.float32) * scale

        @pl.when(part < parts - 1)
        def _():
            rest = pl.multiple_of(part * step + whole, LANES)
            out_ref[:, pl.ds(rest, step - whole)] = ref[:, whole:].astype(jnp.float32) * scale


def join(z, blocks, scale):
    vmem = pl.BlockSpec(memory_space=pltpu.VMEM)
    rows = blocks[0].shape[0]
    return pl.pallas_call(
        functools.partial(join_kernel, scale),
        in_specs=[pl.BlockSpec(memory_space=pltpu.SMEM)] + [vmem] * len(blocks),
        out_specs=vmem,
        out_shape=jax.ShapeDtypeStruct((rows, 3 * WIDTH), jnp.float32),
        compiler_params=pltpu.CompilerParams(vmem_limit_bytes=16 * MIB),
        cost_estimate=pl.CostEstimate(
            flops=rows * 3 * WIDTH, bytes_accessed=6 * rows * 3 * WIDTH, transcendentals=0
        ),
    )(z, *blocks)


def per_device(layer_input, queries, keys, values, d_attn, w_qkv):
    devices = lax.axis_size(SEQ)
    parts = lax.axis_size("z")
    owners = devices // lax.axis_size("core")
    clips = parts * lax.axis_size("xh")
    frames, spatial = layer_input.shape[1], layer_input.shape[2]
    cells = spatial // devices
    rows = devices * frames * cells
    norm_scale = 1.0 / math.sqrt(clips * FRAMES * SPATIAL)
    core = lax.axis_index("core").reshape(1).astype(jnp.int32)

    sent = pack([queries, keys, values, d_attn], devices)
    received = lax.all_to_all(sent, SEQ, 0, 0, tiled=True)
    sent_x = pack([layer_input], devices)
    tokens = lax.all_to_all(sent_x, SEQ, 0, 0, tiled=True).reshape(rows, WIDTH)

    *grads, early = attend(received, w_qkv)
    step = -(-3 * WIDTH // (parts * LANES)) * LANES
    count = parts // 2
    sent_early, turned_own, turned_sent = turn_and_product(
        core, tokens, grads[0], count, step, owners
    )
    sent_late = product(turned_sent, grads[1:], count, step, owners)
    got_early, got_late = swap(sent_early, "core"), swap(sent_late, "core")
    own_part = product(turned_own, grads, parts, step, owners)
    kept = add_parts(own_part, got_early, got_late)
    over_z = lax.psum_scatter(kept, "z", scatter_dimension=0, tiled=True)[0]

    d_local = input_grad(grads, w_qkv, early, kept).reshape(devices, frames, cells, WIDTH)
    d_input = unpack(lax.all_to_all(d_local, SEQ, 0, 0, tiled=True))

    share = fold(lax.all_to_all(over_z, ("y", "xl"), 0, 0, tiled=True), d_input)
    share = add(share, swap(share, "xh"))
    blocks = [share] + [
        lax.ppermute(share, "z", [(i, i ^ n) for i in range(parts)]) for n in range(1, parts)
    ]
    d_weight = join(lax.axis_index("z").reshape(1).astype(jnp.int32), blocks, norm_scale)
    return (d_input, d_weight)


def solution(mesh):
    sizes = (4, 2, 4, 2, 2)
    fine = Mesh(mesh.devices.reshape(sizes), ("z", "xh", "y", "xl", "core"))
    dp = ("z", "xh")
    block = P(dp, SEQ, None, None)
    return jax.shard_map(
        per_device,
        mesh=fine,
        in_specs=(block,) * 5 + (P(),),
        out_specs=(block, P(SEQ, None)),
        check_vma=False,
    )
```

```python
import functools
import math

import jax
import jax.numpy as jnp
from jax import lax
from jax.experimental import pallas as pl
from jax.experimental.pallas import tpu as pltpu
from jax.sharding import Mesh
from jax.sharding import PartitionSpec as P

HEADS = 16
HEAD_DIM = 72
FRAMES = 64
SPATIAL = 256
WIDTH = HEADS * HEAD_DIM
LANES = 128
TILES = WIDTH // LANES
FACTOR = HEAD_DIM ** (-0.5)
SEQ = ("y", "xl", "core")
EARLY_ROWS = 256
SPLIT = 1792
MIB = 1024 * 1024


def pack_kernel(cells, group, *refs):
    out_ref = refs[-1]
    for n, ref in enumerate(refs[:-1]):
        for i in range(group):
            out_ref[i, n] = ref[0, :, i * cells : (i + 1) * cells, :]


def pack(arrays, devices):
    frames, cells = arrays[0].shape[1], arrays[0].shape[2] // devices
    group = 8
    block = pl.BlockSpec((1, frames, group * cells, WIDTH), lambda j: (0, 0, j, 0))
    count = len(arrays)
    return pl.pallas_call(
        functools.partial(pack_kernel, cells, group),
        grid=(devices // group,),
        in_specs=[block] * count,
        out_specs=pl.BlockSpec((group, count, frames, cells, WIDTH), lambda j: (j, 0, 0, 0, 0)),
        out_shape=jax.ShapeDtypeStruct((devices, count, frames, cells, WIDTH), jnp.bfloat16),
        compiler_params=pltpu.CompilerParams(vmem_limit_bytes=60 * MIB),
        cost_estimate=pl.CostEstimate(
            flops=0, bytes_accessed=2 * count * arrays[0].size * 2, transcendentals=0
        ),
    )(*arrays)


def unpack_kernel(cells, group, in_ref, out_ref):
    for i in range(group):
        out_ref[0, :, i * cells : (i + 1) * cells, :] = in_ref[i]


def unpack(blocks):
    devices, frames, cells, width = blocks.shape
    group = 4
    return pl.pallas_call(
        functools.partial(unpack_kernel, cells, group),
        grid=(devices // group,),
        in_specs=[pl.BlockSpec((group, frames, cells, width), lambda j: (j, 0, 0, 0))],
        out_specs=pl.BlockSpec((1, frames, group * cells, width), lambda j: (0, 0, j, 0)),
        out_shape=jax.ShapeDtypeStruct((1, frames, cells * devices, width), jnp.bfloat16),
        compiler_params=pltpu.CompilerParams(vmem_limit_bytes=20 * MIB),
        cost_estimate=pl.CostEstimate(flops=0, bytes_accessed=4 * blocks.size, transcendentals=0),
    )(blocks)


def dot_nt(a, b):
    return lax.dot_general(a, b, (((1,), (1,)), ((), ())), preferred_element_type=jnp.float32)


def dot_tn(a, b):
    return lax.dot_general(a, b, (((0,), (0,)), ((), ())), preferred_element_type=jnp.float32)


def dot_nn(a, b):
    return jnp.dot(a, b, preferred_element_type=jnp.float32)


def attend_kernel(
    cells, r_ref, w_hbm, g0_ref, g1_ref, i_hbm, q_scr, k_scr, v_scr, d_scr, w_scr, i_scr, w_sem, i_sem
):
    w_copy = pltpu.make_async_copy(w_hbm, w_scr, w_sem)
    w_copy.start()
    rows = FRAMES * cells
    scratches = (q_scr, k_scr, v_scr, d_scr)
    for n, scr in enumerate(scratches):
        for t in range(TILES):
            tile = r_ref[:, n, :, :, t * LANES : (t + 1) * LANES]
            scr[t] = tile.reshape(rows, LANES).astype(jnp.float32)

    pair_rows = 2 * FRAMES
    lane = lax.broadcasted_iota(jnp.int32, (FRAMES, 2 * pair_rows), 1)
    left = lane % pair_rows < FRAMES

    def compact(block):
        return jnp.where(left, block[:FRAMES], block[FRAMES:])

    def spread(block):
        zero = jnp.zeros_like(block)
        upper = jnp.where(left, block, zero)
        lower = jnp.where(left, zero, block)
        return jnp.concatenate([upper, lower], axis=0).astype(jnp.bfloat16)

    def pair_step(i, carry):
        p = 2 * i

        def load(scr, t):
            first = scr[t, pl.ds(p, FRAMES, stride=cells), :]
            second = scr[t, pl.ds(p + 1, FRAMES, stride=cells), :]
            return jnp.concatenate([first, second], axis=0).astype(jnp.bfloat16)

        q_t, k_t, v_t, d_t = ([load(scr, t) for t in range(TILES)] for scr in scratches)
        acc = [dict(), dict(), dict()]

        def put(n, t, value):
            acc[n][t] = acc[n][t] + value if t in acc[n] else value

        def scores(h):
            start = h * HEAD_DIM
            first = start // LANES
            low = start - first * LANES
            window_lane = lax.broadcasted_iota(jnp.int32, (1, 2 * LANES), 1)
            masks = [
                ((window_lane >= lo) & (window_lane < lo + HEAD_DIM)).astype(jnp.bfloat16)
                for lo in (low, low + HEAD_DIM)
            ]

            def window(parts):
                return jnp.concatenate([parts[first], parts[first + 1]], axis=1)

            def both(value):
                return jnp.concatenate([value * mask for mask in masks], axis=0)

            k_w = window(k_t)
            q_h = both(window(q_t))
            d_h = both(window(d_t))
            raw = compact(dot_nt(k_w, q_h))
            grad_p = compact(dot_nt(window(v_t), d_h))
            return k_w, q_h, d_h, raw, grad_p

        def soft(k_w, q_h, d_h, raw, grad_p):
            exp_term = jnp.exp((raw - jnp.max(raw, axis=0, keepdims=True)) * FACTOR)
            prob = exp_term * (1.0 / jnp.sum(exp_term, axis=0, keepdims=True))
            prob_low = prob.astype(jnp.bfloat16).astype(jnp.float32)
            delta = jnp.sum(prob_low * grad_p, axis=0, keepdims=True)
            grad_s = spread(prob * (grad_p - delta))
            return k_w, q_h, d_h, spread(prob), grad_s

        def grads(h, k_w, q_h, d_h, prob_low, grad_s):
            start = h * HEAD_DIM
            first = start // LANES
            low = start - first * LANES
            window_lane = lax.broadcasted_iota(jnp.int32, (1, 2 * LANES), 1)
            own = (window_lane >= low) & (window_lane < low + 2 * HEAD_DIM)
            from_keys = dot_tn(grad_s, k_w)
            halves = jnp.where(
                window_lane < low + HEAD_DIM, from_keys[:pair_rows], from_keys[pair_rows:]
            )
            results = (
                jnp.where(own, halves, 0.0),
                dot_nn(grad_s, q_h),
                dot_nn(prob_low, d_h),
            )
            for n, result in enumerate(results):
                put(n, first, result[:, :LANES])
                put(n, first + 1, result[:, LANES:])
            for t in range(first, (start + 2 * HEAD_DIM) // LANES):
                for n, scr in enumerate((q_scr, k_scr, v_scr)):
                    value = acc[n].pop(t)
                    scr[t, pl.ds(p, FRAMES, stride=cells), :] = value[:FRAMES]
                    scr[t, pl.ds(p + 1, FRAMES, stride=cells), :] = value[FRAMES:]

        steps = HEADS // 2
        scored, softened = {}, {}
        for at in range(steps + 2):
            if at < steps:
                scored[at] = scores(2 * at)
            if at >= 2:
                grads(2 * (at - 2), *softened.pop(at - 2))
            if 1 <= at <= steps:
                softened[at - 1] = soft(*scored.pop(at - 1))
        return carry

    lax.fori_loop(0, cells // 2, pair_step, 0)
    for n, scr in enumerate((q_scr, k_scr, v_scr)):
        for t in range(TILES):
            lo = n * WIDTH + t * LANES
            scale = 1.0 if n == 2 else FACTOR
            g_ref, lo = (g0_ref, lo) if lo < SPLIT else (g1_ref, lo - SPLIT)
            g_ref[:, lo : lo + LANES] = (scr[t] * scale).astype(jnp.bfloat16)
    w_copy.wait()
    i_scr[...] = (
        dot_nt(g0_ref[:EARLY_ROWS, :], w_scr[:, :SPLIT])
        + dot_nt(g1_ref[:EARLY_ROWS, :], w_scr[:, SPLIT:])
    ).astype(jnp.bfloat16)
    i_copy = pltpu.make_async_copy(i_scr, i_hbm.at[pl.ds(0, EARLY_ROWS), :], i_sem)
    i_copy.start()
    i_copy.wait()


def attend(received, weight):
    devices, _, frames, cells, _ = received.shape
    rows = devices * frames * cells
    scratch = pltpu.VMEM((TILES, rows, LANES), jnp.float32)
    vmem = pl.BlockSpec(memory_space=pltpu.VMEM)
    return pl.pallas_call(
        functools.partial(attend_kernel, cells),
        in_specs=[vmem, pl.BlockSpec(memory_space=pl.ANY)],
        out_specs=[vmem, vmem, pl.BlockSpec(memory_space=pltpu.HBM)],
        out_shape=[
            jax.ShapeDtypeStruct((rows, SPLIT), jnp.bfloat16),
            jax.ShapeDtypeStruct((rows, 3 * WIDTH - SPLIT), jnp.bfloat16),
            jax.ShapeDtypeStruct((rows, WIDTH), jnp.bfloat16),
        ],
        scratch_shapes=[scratch] * 4
        + [
            pltpu.VMEM(weight.shape, jnp.bfloat16),
            pltpu.VMEM((EARLY_ROWS, WIDTH), jnp.bfloat16),
            pltpu.SemaphoreType.DMA,
            pltpu.SemaphoreType.DMA,
        ],
        compiler_params=pltpu.CompilerParams(vmem_limit_bytes=60 * MIB),
        cost_estimate=pl.CostEstimate(
            flops=24_000_000_000, bytes_accessed=14 * rows * WIDTH, transcendentals=4_000_000
        ),
    )(received, weight)


def input_grad_kernel(g0_ref, g1_ref, w_ref, early_ref, after_ref, out_ref):
    out_ref[...] = (
        dot_nt(g0_ref[...], w_ref[:, :SPLIT]) + dot_nt(g1_ref[...], w_ref[:, SPLIT:])
    ).astype(jnp.bfloat16)


def input_grad(grads, weight, early, after):
    rows, depth = early.shape[0], weight.shape[1]
    step = EARLY_ROWS
    return pl.pallas_call(
        input_grad_kernel,
        grid=(rows // step - 1,),
        in_specs=[
            pl.BlockSpec((step, SPLIT), lambda j: (j + 1, 0)),
            pl.BlockSpec((step, depth - SPLIT), lambda j: (j + 1, 0)),
            pl.BlockSpec((WIDTH, depth), lambda j: (0, 0)),
            pl.BlockSpec(memory_space=pl.ANY),
            pl.BlockSpec(memory_space=pl.ANY),
        ],
        out_specs=pl.BlockSpec((step, WIDTH), lambda j: (j + 1, 0)),
        out_shape=jax.ShapeDtypeStruct((rows, WIDTH), jnp.bfloat16),
        input_output_aliases={3: 0},
        compiler_params=pltpu.CompilerParams(vmem_limit_bytes=60 * MIB),
        cost_estimate=pl.CostEstimate(
            flops=2 * rows * depth * WIDTH,
            bytes_accessed=2 * depth * (rows + WIDTH),
            transcendentals=0,
        ),
    )(*grads, weight, early, after)


def multiply(turned, g_ref, out_ref, first):
    owners, share, step = out_ref.shape[1:]
    wide = dot_nn(turned, g_ref[...])
    width = wide.shape[1]
    for n in range(-(-width // step)):
        end = min(step, width - n * step)
        for block in range(owners):
            piece = wide[block * share : (block + 1) * share, n * step : n * step + end]
            out_ref[first + n, block, :, :end] = piece.astype(jnp.bfloat16)
        if end < step:
            out_ref[first + n, :, :, end:] = jnp.zeros((owners, share, step - end), jnp.bfloat16)


def turn_kernel(core_ref, x_hbm, g_ref, out_ref, own_ref, sent_ref, x_scr, wide_scr, x_sems):
    chunks, rows = x_scr.shape[:2]
    share = out_ref.shape[2]
    x_copies = [
        pltpu.make_async_copy(x_hbm.at[pl.ds(i * rows, rows), :], x_scr.at[i], x_sems.at[i])
        for i in range(chunks)
    ]
    for copy in x_copies:
        copy.start()
    for i, copy in enumerate(x_copies):
        copy.wait()
        flipped = x_scr[i].astype(jnp.float32).T
        for n, turned_ref in enumerate((own_ref, sent_ref)):
            for block in range(out_ref.shape[1]):
                lo = 2 * block * share
                even, odd = flipped[lo : lo + share], flipped[lo + share : lo + 2 * share]
                wide_scr[n, block * share : (block + 1) * share, :] = jnp.where(
                    core_ref[0] == n, even, odd
                )
            turned_ref[:, i * rows : (i + 1) * rows] = wide_scr[n].astype(jnp.bfloat16)
    multiply(sent_ref[...], g_ref, out_ref, 0)


def product_kernel(turned_ref, *refs):
    out_ref = refs[-1]
    first = 0
    for g_ref in refs[:-1]:
        multiply(turned_ref[...], g_ref, out_ref, first)
        first += g_ref.shape[1] // out_ref.shape[3]


def turn_and_product(core, tokens, grads, parts, step, owners):
    rows, chunks = tokens.shape[0], 4
    half = WIDTH // 2
    vmem = pl.BlockSpec(memory_space=pltpu.VMEM)
    hbm = pl.BlockSpec(memory_space=pltpu.HBM)
    turned = jax.ShapeDtypeStruct((half, rows), jnp.bfloat16)
    return pl.pallas_call(
        turn_kernel,
        in_specs=[pl.BlockSpec(memory_space=pltpu.SMEM), hbm, vmem],
        out_specs=[vmem, vmem, vmem],
        out_shape=[
            jax.ShapeDtypeStruct((parts, owners, half // owners, step), jnp.bfloat16),
            turned,
            turned,
        ],
        scratch_shapes=[
            pltpu.VMEM((chunks, rows // chunks, WIDTH), jnp.bfloat16),
            pltpu.VMEM((2, half, rows // chunks), jnp.float32),
            pltpu.SemaphoreType.DMA((chunks,)),
        ],
        compiler_params=pltpu.CompilerParams(vmem_limit_bytes=24 * MIB),
        cost_estimate=pl.CostEstimate(
            flops=rows * WIDTH * step * parts,
            bytes_accessed=rows * (2 * WIDTH + 2 * step * parts) + WIDTH * step * parts,
            transcendentals=0,
        ),
    )(core, tokens, grads)


def product(turned, ranges, parts, step, owners):
    half, rows = turned.shape
    vmem = pl.BlockSpec(memory_space=pltpu.VMEM)
    return pl.pallas_call(
        product_kernel,
        in_specs=[vmem] * (1 + len(ranges)),
        out_specs=vmem,
        out_shape=jax.ShapeDtypeStruct((parts, owners, half // owners, step), jnp.bfloat16),
        compiler_params=pltpu.CompilerParams(vmem_limit_bytes=24 * MIB),
        cost_estimate=pl.CostEstimate(
            flops=rows * WIDTH * step * parts,
            bytes_accessed=rows * (WIDTH + 2 * step * parts) + WIDTH * step * parts,
            transcendentals=0,
        ),
    )(turned, *ranges)


def add_kernel(own_ref, early_ref, late_ref, out_ref):
    half = pl.num_programs(0) // 2
    at = pl.program_id(0)

    @pl.when(at < half)
    def _():
        out_ref[...] = add(own_ref[...], early_ref[...])

    @pl.when(at >= half)
    def _():
        out_ref[...] = add(own_ref[...], late_ref[...])


def add_parts(own, early, late):
    parts = own.shape[0]
    half = parts // 2
    block = (1,) + own.shape[1:]
    return pl.pallas_call(
        add_kernel,
        grid=(parts,),
        in_specs=[
            pl.BlockSpec(block, lambda j: (j, 0, 0, 0)),
            pl.BlockSpec(block, lambda j: (jnp.minimum(j, half - 1), 0, 0, 0)),
            pl.BlockSpec(block, lambda j: (jnp.maximum(j - half, 0), 0, 0, 0)),
        ],
        out_specs=pl.BlockSpec(block, lambda j: (j, 0, 0, 0)),
        out_shape=jax.ShapeDtypeStruct(own.shape, own.dtype),
        compiler_params=pltpu.CompilerParams(vmem_limit_bytes=24 * MIB),
        cost_estimate=pl.CostEstimate(
            flops=own.size, bytes_accessed=6 * own.size, transcendentals=0
        ),
    )(own, early, late)


def swap(value, axis):
    return lax.ppermute(value, axis, [(0, 1), (1, 0)])


def add(first, second):
    return (first.astype(jnp.float32) + second.astype(jnp.float32)).astype(jnp.bfloat16)


def fold_kernel(blocks_ref, after_ref, out_ref):
    total = blocks_ref[0].astype(jnp.float32)
    for n in range(1, blocks_ref.shape[0]):
        total = total + blocks_ref[n].astype(jnp.float32)
    out_ref[...] = total.astype(jnp.bfloat16)


def fold(blocks, after):
    vmem = pl.BlockSpec(memory_space=pltpu.VMEM)
    return pl.pallas_call(
        fold_kernel,
        in_specs=[vmem, pl.BlockSpec(memory_space=pl.ANY)],
        out_specs=vmem,
        out_shape=jax.ShapeDtypeStruct(blocks.shape[1:], jnp.bfloat16),
        compiler_params=pltpu.CompilerParams(vmem_limit_bytes=16 * MIB),
        cost_estimate=pl.CostEstimate(
            flops=blocks.size, bytes_accessed=2 * blocks.size, transcendentals=0
        ),
    )(blocks, after)


def join_kernel(scale, z_ref, *refs):
    out_ref = refs[-1]
    parts = len(refs) - 1
    step = refs[0].shape[1]
    whole = out_ref.shape[1] - (parts - 1) * step
    for n, ref in enumerate(refs[:-1]):
        part = z_ref[0] ^ n
        lo = pl.multiple_of(part * step, LANES)
        out_ref[:, pl.ds(lo, whole)] = ref[:, :whole].astype(jnp.float32) * scale

        @pl.when(part < parts - 1)
        def _():
            rest = pl.multiple_of(part * step + whole, LANES)
            out_ref[:, pl.ds(rest, step - whole)] = ref[:, whole:].astype(jnp.float32) * scale


def join(z, blocks, scale):
    vmem = pl.BlockSpec(memory_space=pltpu.VMEM)
    rows = blocks[0].shape[0]
    return pl.pallas_call(
        functools.partial(join_kernel, scale),
        in_specs=[pl.BlockSpec(memory_space=pltpu.SMEM)] + [vmem] * len(blocks),
        out_specs=vmem,
        out_shape=jax.ShapeDtypeStruct((rows, 3 * WIDTH), jnp.float32),
        compiler_params=pltpu.CompilerParams(vmem_limit_bytes=16 * MIB),
        cost_estimate=pl.CostEstimate(
            flops=rows * 3 * WIDTH, bytes_accessed=6 * rows * 3 * WIDTH, transcendentals=0
        ),
    )(z, *blocks)


def per_device(layer_input, queries, keys, values, d_attn, w_qkv):
    devices = lax.axis_size(SEQ)
    parts = lax.axis_size("z")
    owners = devices // lax.axis_size("core")
    clips = parts * lax.axis_size("xh")
    frames, spatial = layer_input.shape[1], layer_input.shape[2]
    cells = spatial // devices
    rows = devices * frames * cells
    norm_scale = 1.0 / math.sqrt(clips * FRAMES * SPATIAL)
    core = lax.axis_index("core").reshape(1).astype(jnp.int32)

    sent = pack([queries, keys, values, d_attn], devices)
    received = lax.all_to_all(sent, SEQ, 0, 0, tiled=True)
    sent_x = pack([layer_input], devices)
    tokens = lax.all_to_all(sent_x, SEQ, 0, 0, tiled=True).reshape(rows, WIDTH)

    *grads, early = attend(received, w_qkv)
    step = -(-3 * WIDTH // (parts * LANES)) * LANES
    count = parts // 2
    sent_early, turned_own, turned_sent = turn_and_product(
        core, tokens, grads[0], count, step, owners
    )
    sent_late = product(turned_sent, grads[1:], count, step, owners)
    got_early, got_late = swap(sent_early, "core"), swap(sent_late, "core")
    own_part = product(turned_own, grads, parts, step, owners)
    kept = add_parts(own_part, got_early, got_late)
    over_z = lax.psum_scatter(kept, "z", scatter_dimension=0, tiled=True)[0]

    d_local = input_grad(grads, w_qkv, early, kept).reshape(devices, frames, cells, WIDTH)
    d_input = unpack(lax.all_to_all(d_local, SEQ, 0, 0, tiled=True))

    share = fold(lax.all_to_all(over_z, ("y", "xl"), 0, 0, tiled=True), d_input)
    share = add(share, swap(share, "xh"))
    blocks = [share] + [
        lax.ppermute(share, "z", [(i, i ^ n) for i in range(parts)]) for n in range(1, parts)
    ]
    d_weight = join(lax.axis_index("z").reshape(1).astype(jnp.int32), blocks, norm_scale)
    return (d_input, d_weight)


def solution(mesh):
    sizes = (4, 2, 4, 2, 2)
    fine = Mesh(mesh.devices.reshape(sizes), ("z", "xh", "y", "xl", "core"))
    dp = ("z", "xh")
    block = P(dp, SEQ, None, None)
    return jax.shard_map(
        per_device,
        mesh=fine,
        in_specs=(block,) * 5 + (P(),),
        out_specs=(block, P(SEQ, None)),
        check_vma=False,
    )
```
